512 devices in a mesh: seq: 128 (over y, x, z_lo), slide: 4 (over z_hi, core).
Axes of the slice: x: 4, y: 4, z: 16 (z_hi: 2, z_lo: 8; z = z_hi * 8 + z_lo), core: 2. Of those that a mesh axis runs over, the one named last changes fastest.
Arguments:
- tiles: bfloat16 [4, 16384, 1536], P('slide', 'seq'), may hold values from -25 to 25
- counts: int32 [4, 128], P('slide', 'seq'), may hold values from 1 to 128
- w_in: bfloat16 [1536, 768], P('slide'), may hold values from -0.15625 to 0.15625
- w_qkv: bfloat16 [768, 2304], P(None, 'slide'), may hold values from -0.5 to 0.5
- w_out: bfloat16 [768, 768], P(None, 'slide'), may hold values from -0.21875 to 0.21875
- cotangent: bfloat16 [4, 16384, 768], P('slide', 'seq'), may hold values from -6 to 6
Outputs:
- slide_out: float32 [4, 16384, 768], P('slide', 'seq')
- grad_out: float32 [768, 768], P('slide')
The draws below stay inside these ranges and needn't reach their ends.
Inputs may be any that keep to these rules, and one draw needn't show every extreme that they name: `counts`: every device holds at least one tissue tile, in its first slots.
All inputs are finite; a program needn't handle non-finite values.
Results may differ from the reference program's by a relative error of at most 0.0095.
Values may be sent and summed in bfloat16 or wider, within the bound.
No kernel may reach another device: no remote copies, remote signals or barrier semaphores. Data moves between devices by JAX's collectives and lax.ppermute only.
A program may use at most 64 MiB of HBM per device.

```python
import jax
import jax.numpy as jnp
from jax import lax

D_TILE = 1536
ENCODER_WIDTH = 768
HEADS = 16
HEAD = 48
SLIDE_DILATION = 32
TOK_DEV = 128
TILE_TOKENS = 16384
SLIDES = 4
N_SEQ = 128


def draw_tiles(key, part):
    key = jax.random.fold_in(key, 11)
    first = jax.random.fold_in(key, 0)
    shape = (SLIDES, TILE_TOKENS, D_TILE)
    result = jnp.clip(jax.random.normal(first, shape, jnp.float32), -6.0, 6.0)
    return result.astype(jnp.bfloat16)


def draw_w_qkv(key, part):
    key = jax.random.fold_in(key, 23)
    first = jax.random.fold_in(key, 0)
    factor = ENCODER_WIDTH ** (-0.5)
    result = jnp.clip(jax.random.normal(first, (ENCODER_WIDTH, 3 * ENCODER_WIDTH), jnp.float32), -4.0, 4.0) * factor
    return result.astype(jnp.bfloat16)


def plant(values, own_key, smallest, top_value):
    longest = values.shape.index(max(values.shape))
    spots = []
    for shift in (0, 1):
        where = [jax.random.randint(jax.random.fold_in(own_key, axis), (), 0, length) for axis, length in enumerate(values.shape)]
        where[longest] = (where[longest] + shift) % values.shape[longest]
        spots.append(tuple(where))
    return values.at[spots[0]].set(smallest).at[spots[1]].set(top_value)


def levels(stream_key, shape, cuts, least, largest):
    def one(position, parts):
        draws = jax.random.uniform(jax.random.fold_in(jax.random.fold_in(stream_key, 6), position), (parts,), jnp.float32, least / len(cuts), largest / len(cuts))
        return jnp.repeat(jnp.exp(draws), shape[position] // parts).reshape((-1,) + (1,) * (len(shape) - position - 1))

    gain = one(*cuts[0])
    for cut in cuts[1:]:
        gain = gain * one(*cut)
    return gain


def noise(stream_key, dims, scale, bound, shards=(), kind=jnp.bfloat16):
    entries = scale * jax.random.normal(stream_key, dims, jnp.float32)
    if shards:
        entries = entries * levels(stream_key, dims, shards, -0.22, 0.18)
    return jnp.clip(entries, -bound, bound).astype(kind)


def setup_inputs(seed: int = 0) -> dict:
    splits = jax.random.split(jax.random.key(seed), 7)
    tiles = draw_tiles(jax.random.fold_in(splits[6], 71), 0)
    counts = plant(jax.random.randint(splits[1], (SLIDES, N_SEQ), 1, TOK_DEV + 1), jax.random.fold_in(splits[1], 1), 1, TOK_DEV).astype(jnp.int32)
    w_in = noise(splits[2], (D_TILE, ENCODER_WIDTH), D_TILE ** -0.5, 0.15625, ((0, 4),))
    w_qkv = draw_w_qkv(jax.random.fold_in(splits[6], 71), 0)
    w_out = noise(splits[4], (ENCODER_WIDTH, ENCODER_WIDTH), ENCODER_WIDTH ** -0.5, 0.21875, ((1, 4),))
    cotangent = noise(splits[5], (SLIDES, TILE_TOKENS, ENCODER_WIDTH), 1.0, 6.0, ((0, 4), (1, 128)))
    return {"tiles": tiles, "counts": counts, "w_in": w_in, "w_qkv": w_qkv, "w_out": w_out, "cotangent": cotangent}


def attend_block(query, key_matrix, value_matrix, valid_mask):
    qh = query.reshape(query.shape[0], HEADS, HEAD).astype(jnp.float32)
    kh = key_matrix.reshape(key_matrix.shape[0], HEADS, HEAD).astype(jnp.float32)
    vh = value_matrix.reshape(value_matrix.shape[0], HEADS, HEAD).astype(jnp.float32)
    scores = jnp.einsum("thd,khd->thk", qh, kh) * (HEAD ** -0.5)
    scores = jnp.where(valid_mask[None, None, :] > 0, scores, jnp.float32(-1e30))
    top = jnp.max(scores, axis=-1, keepdims=True)
    weights = jnp.exp(scores - top)
    total = jnp.sum(weights, axis=-1)
    mixed = jnp.einsum("thk,khd->thd", weights.astype(jnp.bfloat16).astype(jnp.float32), vh)
    return (mixed / total[..., None]).reshape(query.shape[0], ENCODER_WIDTH).astype(jnp.bfloat16)


def one_slide(rows, count_row, w_in, w_qkv, w_out, cot):
    hidden = jnp.dot(rows, w_in, preferred_element_type=jnp.float32).astype(jnp.bfloat16)
    qkv = jnp.dot(hidden, w_qkv, preferred_element_type=jnp.float32).astype(jnp.bfloat16)
    query, key_matrix, value_matrix = qkv[:, :ENCODER_WIDTH], qkv[:, ENCODER_WIDTH:2 * ENCODER_WIDTH], qkv[:, 2 * ENCODER_WIDTH:]
    offset = jnp.arange(TILE_TOKENS, dtype=jnp.int32) % TOK_DEV
    block_id = jnp.arange(TILE_TOKENS, dtype=jnp.int32) // TOK_DEV
    valid_mask = (offset < count_row[block_id]).astype(jnp.float32)
    distant_keys = key_matrix.reshape(TILE_TOKENS // SLIDE_DILATION, SLIDE_DILATION, ENCODER_WIDTH)[:, 0]
    distant_values = value_matrix.reshape(TILE_TOKENS // SLIDE_DILATION, SLIDE_DILATION, ENCODER_WIDTH)[:, 0]
    distant_mask = valid_mask.reshape(TILE_TOKENS // SLIDE_DILATION, SLIDE_DILATION)[:, 0]

    def per_block(index):
        start = (index * TOK_DEV).astype(jnp.int32)
        pstart = ((index ^ 1) * TOK_DEV).astype(jnp.int32)
        q_b = lax.dynamic_slice_in_dim(query, start, TOK_DEV, 0)
        k_b = lax.dynamic_slice_in_dim(key_matrix, start, TOK_DEV, 0)
        v_b = lax.dynamic_slice_in_dim(value_matrix, start, TOK_DEV, 0)
        m_b = lax.dynamic_slice_in_dim(valid_mask, start, TOK_DEV, 0)
        k_p = lax.dynamic_slice_in_dim(key_matrix, pstart, TOK_DEV, 0)
        v_p = lax.dynamic_slice_in_dim(value_matrix, pstart, TOK_DEV, 0)
        m_p = lax.dynamic_slice_in_dim(valid_mask, pstart, TOK_DEV, 0)
        all_k = jnp.concatenate([k_b, k_b[0::2], k_p[0::2], distant_keys], axis=0)
        all_v = jnp.concatenate([v_b, v_b[0::2], v_p[0::2], distant_values], axis=0)
        all_m = jnp.concatenate([m_b, m_b[0::2], m_p[0::2], distant_mask], axis=0)
        return attend_block(q_b, all_k, all_v, all_m)

    attn = lax.map(per_block, jnp.arange(N_SEQ, dtype=jnp.int32)).reshape(TILE_TOKENS, ENCODER_WIDTH)
    out = jnp.dot(attn, w_out, preferred_element_type=jnp.float32)
    masked = jnp.where(valid_mask[:, None] > 0, attn, jnp.zeros_like(attn))
    grad = jnp.dot(masked.T, cot, preferred_element_type=jnp.float32)
    return out, grad


def reference(tiles, counts, w_in, w_qkv, w_out, cotangent):
    outs = []
    grad_out = jnp.zeros((ENCODER_WIDTH, ENCODER_WIDTH), jnp.float32)
    for index in range(SLIDES):
        out, grad = one_slide(tiles[index], counts[index], w_in, w_qkv, w_out, cotangent[index])
        outs.append(out)
        grad_out = grad_out + grad
    return jnp.stack(outs, axis=0), grad_out
```

```python
import functools

import jax
import jax.numpy as jnp
from jax import lax
from jax.experimental import pallas as pl
from jax.experimental.pallas import tpu as pltpu
from jax.sharding import Mesh
from jax.sharding import PartitionSpec as P

WIDTH = 768
HEADS = 16
HEAD = 48
DIL = 32
TOK = 128
PIECE = 64
YX = ("y", "x")
NT = (((1,), (1,)), ((), ()))
NN = (((1,), (0,)), ((), ()))
BF = jnp.bfloat16
F32 = jnp.float32


def layer_kernel(
    scal,
    rows,
    even,
    partner,
    w_in,
    w_qkv,
    mate_in,
    mate_qkv,
    got,
    cross,
    w_out,
    cot,
    out,
    keep,
    send,
    near,
    far,
    marks,
    win,
    wqkv,
    hid,
    kv,
    mixed,
    attn,
    sems,
):
    count, pcount, zh, core = scal[0], scal[1], scal[2], scal[3]
    mine = zh * 2 + core
    mate = zh * 2 + 1 - core
    over = (1 - zh) * 2 + core
    over_mate = (1 - zh) * 2 + 1 - core
    moves = [
        (rows, near.at[pl.ds(0, TOK)]),
        (even, near.at[pl.ds(TOK, TOK // 2)]),
        (partner, near.at[pl.ds(TOK + TOK // 2, TOK // 2)]),
        (got.at[:, pl.ds(PIECE, 64)], far),
        (got.at[:, pl.ds(PIECE + 64, 16)], marks),
        (w_in, win.at[mine]),
        (mate_in, win.at[mate]),
        (got.at[pl.ds(0, 6), pl.ds(0, PIECE)], win.at[over]),
        (cross.at[pl.ds(0, 6)], win.at[over_mate]),
        (w_qkv, wqkv.at[mine]),
        (mate_qkv, wqkv.at[mate]),
        (got.at[pl.ds(6, 9), pl.ds(0, PIECE)], wqkv.at[over]),
        (cross.at[pl.ds(6, 9)], wqkv.at[over_mate]),
    ]
    copies = [pltpu.make_async_copy(s, d, sems.at[i]) for i, (s, d) in enumerate(moves)]
    for c in copies:
        c.start()
    for c in copies[:9]:
        c.wait()
    weight = win[...].reshape(1536, WIDTH)
    hid[pl.ds(0, 256), :] = lax.dot_general(
        near[...], weight, NN, preferred_element_type=F32
    ).astype(BF)
    left = far[:, pl.ds(0, 32), :].reshape(512, WIDTH)
    right = far[:, pl.ds(32, 32), :].reshape(512, WIDTH)
    hid[pl.ds(256, 512), :] = (
        lax.dot_general(left, weight[:WIDTH], NN, preferred_element_type=F32)
        + lax.dot_general(right, weight[WIDTH:], NN, preferred_element_type=F32)
    ).astype(BF)
    for c in copies[9:]:
        c.wait()
    kv[...] = lax.dot_general(
        wqkv[...].reshape(3 * WIDTH, WIDTH)[WIDTH:], hid[...], NT, preferred_element_type=F32
    ).astype(BF)
    seen = jnp.sum(marks[...].astype(F32), axis=(0, 1)).reshape(1, WIDTH)[:, :512]
    lane = lax.broadcasted_iota(jnp.int32, (1, 256), 1)
    offset = jnp.where(lane < TOK, lane, 2 * (lane & 63))
    limit = jnp.where(lane < TOK + TOK // 2, count, pcount)
    near_bias = jnp.where(offset < limit, F32(0), F32(-1e30))
    far_bias = jnp.where(seen > 0.5, F32(0), F32(-1e30))
    bias = jnp.concatenate([near_bias, far_bias], axis=1)
    column = lax.broadcasted_iota(jnp.int32, (TOK, TOK), 1)
    totals = jnp.ones((TOK, TOK), F32)
    own = hid[pl.ds(0, TOK), :]
    flat = wqkv[...].reshape(3 * WIDTH, WIDTH)
    for h in range(HEADS):
        q = lax.dot_general(
            own, flat[h * HEAD : (h + 1) * HEAD], NT, preferred_element_type=F32
        ).astype(BF)
        s = lax.dot_general(
            q, kv[pl.ds(h * HEAD, HEAD), :], NN, preferred_element_type=F32
        )
        s = s * F32(HEAD**-0.5) + bias
        top = jnp.max(s, axis=1, keepdims=True)
        p = jnp.exp(s - top)
        totals = jnp.where(column == h, jnp.sum(p, axis=1, keepdims=True), totals)
        mixed[pl.ds(h * HEAD, HEAD), :] = lax.dot_general(
            kv[pl.ds(WIDTH + h * HEAD, HEAD), :], p.astype(BF), NT, preferred_element_type=F32
        )
    inverse = 1.0 / totals.T
    for h in range(HEADS):
        attn[pl.ds(h * HEAD, HEAD), :] = (
            mixed[pl.ds(h * HEAD, HEAD), :] * inverse[h : h + 1, :]
        ).astype(BF)
    cotangent = cot[...]
    token = lax.broadcasted_iota(jnp.int32, (192, TOK), 1)
    for which, target in ((core, keep), (1 - core, send)):
        for half in range(2):
            start = pl.multiple_of(half * 384 + which * 192, 192)
            block = attn[pl.ds(start, 192), :]
            block = jnp.where(token < count, block, jnp.zeros_like(block))
            part = lax.dot_general(block, cotangent, NN, preferred_element_type=F32)
            for r in range(8):
                for c in range(2):
                    target[r * 2 + c, half] = part[r * 24 : r * 24 + 24, c * 384 : c * 384 + 384]
    out_t = lax.dot_general(w_out[...], attn[...], NN, preferred_element_type=F32)
    out[...] = out_t.T


def layer(*operands, interpret=False):
    any_spec = pl.BlockSpec(memory_space=pl.ANY)
    vmem = pl.BlockSpec(memory_space=pltpu.VMEM)
    part = jax.ShapeDtypeStruct((16, 2, 24, 384), F32)
    return pl.pallas_call(
        layer_kernel,
        out_shape=(jax.ShapeDtypeStruct((TOK, WIDTH), F32), part, part),
        in_specs=[pl.BlockSpec(memory_space=pltpu.SMEM)] + [any_spec] * 9 + [vmem] * 2,
        out_specs=(vmem, vmem, vmem),
        scratch_shapes=[
            pltpu.VMEM((256, 1536), BF),
            pltpu.VMEM((16, 64, WIDTH), BF),
            pltpu.VMEM((16, 16, WIDTH), BF),
            pltpu.VMEM((4, 6, PIECE, WIDTH), BF),
            pltpu.VMEM((4, 9, PIECE, WIDTH), BF),
            pltpu.VMEM((WIDTH, WIDTH), BF),
            pltpu.VMEM((2 * WIDTH, WIDTH), BF),
            pltpu.VMEM((WIDTH, TOK), F32),
            pltpu.VMEM((WIDTH, TOK), BF),
            pltpu.SemaphoreType.DMA((13,)),
        ],
        compiler_params=pltpu.CompilerParams(vmem_limit_bytes=48 * 1024 * 1024),
        interpret=interpret,
    )(*operands)


def spread(block, axes, size):
    return lax.all_to_all(
        jnp.broadcast_to(block[None], (size,) + block.shape), axes, 0, 0, tiled=True
    )


def swap(value, axis):
    return lax.ppermute(value, axis, [(0, 1), (1, 0)])


def shards(tiles, counts, w_in, w_qkv, w_out, cotangent):
    rows = tiles[0]
    count = counts[0, 0]
    yx = lax.axis_index("y") * 4 + lax.axis_index("x")
    zl, zh, core = lax.axis_index("zl"), lax.axis_index("zh"), lax.axis_index("core")
    w_in = w_in.reshape(6, PIECE, WIDTH)
    w_qkv = w_qkv.T.reshape(9, PIECE, WIDTH)
    piece = jnp.where(
        yx < 6,
        lax.dynamic_index_in_dim(w_in, jnp.minimum(yx, 5), 0, False),
        lax.dynamic_index_in_dim(w_qkv, jnp.clip(yx - 6, 0, 8), 0, False),
    )
    piece = swap(piece, "zh")
    even = rows[0::2]
    partner = lax.ppermute(even, "zl", [(i, i ^ 1) for i in range(8)])
    mate_in, mate_qkv = swap(w_in, "core"), swap(w_qkv, "core")
    out_w = lax.all_gather(w_out.T, ("zh", "core"), axis=0, tiled=True)
    distant = rows[0::DIL]
    lane = lax.broadcasted_iota(jnp.int32, (1, WIDTH), 1)
    local = lane - (yx * 32 + zl * 4)
    mark = (local >= 0) & (local < 4) & (local * DIL < count)
    mark = jnp.where(lane == 512, count.astype(BF), mark.astype(BF))
    block = jnp.concatenate(
        [distant[:, :WIDTH], distant[:, WIDTH:], mark, jnp.zeros((7, WIDTH), BF)], axis=0
    )
    line = spread(block, "zl", 8)
    pcount = lax.dynamic_slice(line, (zl ^ 1, 8, 512), (1, 1, 1))[0, 0, 0].astype(jnp.int32)
    payload = jnp.concatenate(
        [
            piece,
            line[:, 0:4].reshape(32, WIDTH),
            line[:, 4:8].reshape(32, WIDTH),
            line[:, 8],
            jnp.zeros((8, WIDTH), BF),
        ],
        axis=0,
    )
    got = spread(payload, YX, 16)
    cross = swap(got[:15, :PIECE], "core")
    scal = jnp.stack([count, pcount, zh, core]).astype(jnp.int32)
    out, keep, send = layer(
        scal, rows, even, partner, w_in, w_qkv, mate_in, mate_qkv, got, cross, out_w, cotangent[0]
    )
    pair = (keep + swap(send, "core")).astype(BF)
    plane = lax.all_to_all(pair, YX, 0, 0, tiled=True)
    plane = jnp.sum(plane.astype(F32), axis=0).astype(BF)
    column = jnp.broadcast_to(plane[:, None], (2, 8, 24, 384)).reshape(16, 24, 384)
    column = lax.all_to_all(column, ("zh", "zl"), 0, 0, tiled=True)
    total = jnp.sum(column.astype(F32), axis=0)
    whole = spread(total, YX, 16)
    grad = whole.reshape(8, 2, 24, 384).transpose(0, 2, 1, 3).reshape(192, WIDTH)
    return (out[None], grad)


def solution(mesh):
    fine = Mesh(mesh.devices.reshape(4, 4, 8, 2, 2), ("y", "x", "zl", "zh", "core"))
    seq, slide = ("y", "x", "zl"), ("zh", "core")
    placed = (
        P(slide, seq, None),
        P(slide, seq),
        P(slide, None),
        P(None, slide),
        P(None, slide),
        P(slide, seq, None),
    )
    return jax.shard_map(
        shards,
        mesh=fine,
        in_specs=placed,
        out_specs=(P(slide, seq, None), P(slide, None)),
        check_vma=False,
    )
```

```python
import jax
import jax.numpy as jnp
from jax import lax
from jax.experimental import pallas as pl
from jax.experimental.pallas import tpu as pltpu
from jax.sharding import Mesh
from jax.sharding import PartitionSpec as P

WIDTH = 768
TILE = 1536
HEADS = 16
HEAD = 48
DIL = 32
TOK = 128
FAR = 512
PACK = 1152
YX = ("y", "x")
NT = (((1,), (1,)), ((), ()))
NN = (((1,), (0,)), ((), ()))
BF = jnp.bfloat16
F32 = jnp.float32
MARK = 64.0
LOW = -1e30
VMEM_BYTES = 56 * 1024 * 1024


def dot(a, b, dims):
    return lax.dot_general(a, b, dims, preferred_element_type=F32)


def weight_moves(scal, packs, win, wqkv):
    zh, core = scal[1], scal[2]
    places = (zh * 2 + core, zh * 2 + 1 - core, (1 - zh) * 2 + core, (1 - zh) * 2 + 1 - core)
    first = [(p.at[pl.ds(0, 384)], win.at[s]) for p, s in zip(packs, places)]
    second = [(p.at[pl.ds(384, 576)], wqkv.at[s]) for p, s in zip(packs, places)]
    return first, second


def key_bias(block):
    lane = lax.broadcasted_iota(jnp.int32, (16, TOK), 1)
    pick = jnp.where(lane == 0, F32(1), F32(0)).astype(BF)
    return jnp.where(dot(pick, block[:, :TOK], NT)[0:1] > MARK / 2, F32(LOW), F32(0))


def attend(query, kv, bias, mixed):
    column = lax.broadcasted_iota(jnp.int32, (TOK, TOK), 1)
    tops = jnp.zeros((TOK, TOK), F32)
    totals = jnp.ones((TOK, TOK), F32)
    for h in range(HEADS):
        s = dot(query(h), kv[pl.ds(h * HEAD, HEAD), :], NN) * F32(HEAD**-0.5) + bias
        top = jnp.max(s, axis=1, keepdims=True)
        p = jnp.exp(s - top)
        tops = jnp.where(column == h, top, tops)
        totals = jnp.where(column == h, jnp.sum(p, axis=1, keepdims=True), totals)
        mixed[pl.ds(h * HEAD, HEAD), :] = dot(
            kv[pl.ds(WIDTH + h * HEAD, HEAD), :], p.astype(BF), NT
        )
    return tops.T, totals.T


def near_kernel(
    scal, rows, even, partner, own, mate, got, cross, query, mixed, tops, totals, near, win, wqkv, hid, kv, sems
):
    first, second = weight_moves(scal, (own, mate, got, cross), win, wqkv)
    moves = [
        (rows, near.at[pl.ds(0, TOK)]),
        (even, near.at[pl.ds(TOK, TOK // 2)]),
        (partner, near.at[pl.ds(TOK + TOK // 2, TOK // 2)]),
    ]
    moves = moves + first + second
    copies = [pltpu.make_async_copy(s, d, sems.at[i]) for i, (s, d) in enumerate(moves)]
    for c in copies:
        c.start()
    for c in copies[:7]:
        c.wait()
    hid[...] = dot(near[...], win[...].reshape(TILE, WIDTH), NN).astype(BF)
    for c in copies[7:]:
        c.wait()
    flat = wqkv[...].reshape(3 * WIDTH, WIDTH)
    kv[...] = dot(flat[WIDTH:], hid[...], NT).astype(BF)
    own_hid = hid[pl.ds(0, TOK), :]
    for h in range(HEADS):
        query[h] = dot(own_hid, flat[h * HEAD : (h + 1) * HEAD], NT).astype(BF)
    lane = lax.broadcasted_iota(jnp.int32, (1, 192), 1)
    offset = jnp.where(lane < TOK, lane, 2 * (lane - TOK))
    mine = jnp.where(offset < scal[0], F32(0), F32(LOW))
    bias = jnp.concatenate([mine, key_bias(near[pl.ds(192, 64), :])], axis=1)
    tops[...], totals[...] = attend(lambda h: query[h], kv, bias, mixed)


def far_kernel(
    scal,
    rows,
    query,
    near_mixed,
    near_tops,
    near_totals,
    cot,
    own,
    mate,
    got,
    cross,
    out,
    keep,
    send,
    far,
    win,
    wqkv,
    wout,
    hid,
    kv,
    mixed,
    attn,
    sems,
):
    first, second = weight_moves(scal, (own, mate, got, cross), win, wqkv)
    zh, core = scal[1], scal[2]
    places = (zh * 2 + core, zh * 2 + 1 - core, (1 - zh) * 2 + core, (1 - zh) * 2 + 1 - core)
    last = [(p.at[pl.ds(960, 192)], wout.at[s]) for p, s in zip((own, mate, got, cross), places)]
    moves = [(rows, far)] + first + second + last
    copies = [pltpu.make_async_copy(s, d, sems.at[i]) for i, (s, d) in enumerate(moves)]
    for c in copies:
        c.start()
    for c in copies[:5]:
        c.wait()
    left = far[:, pl.ds(0, 32), :].reshape(FAR, WIDTH)
    right = far[:, pl.ds(32, 32), :].reshape(FAR, WIDTH)
    weight = win[...].reshape(TILE, WIDTH)
    hid[...] = (dot(left, weight[:WIDTH], NN) + dot(right, weight[WIDTH:], NN)).astype(BF)
    for c in copies[5:]:
        c.wait()
    kv[...] = dot(wqkv[...].reshape(3 * WIDTH, WIDTH)[WIDTH:], hid[...], NT).astype(BF)
    far_tops, far_totals = attend(lambda h: query[h], kv, key_bias(left), mixed)
    top = jnp.maximum(near_tops[...], far_tops)
    near_scale, far_scale = jnp.exp(near_tops[...] - top), jnp.exp(far_tops - top)
    inverse = 1.0 / (near_totals[...] * near_scale + far_totals * far_scale)
    near_scale, far_scale = near_scale * inverse, far_scale * inverse
    for h in range(HEADS):
        at = pl.ds(h * HEAD, HEAD)
        attn[at, :] = (
            near_mixed[at, :] * near_scale[h : h + 1, :] + mixed[at, :] * far_scale[h : h + 1, :]
        ).astype(BF)
    cotangent = cot[...]
    token = lax.broadcasted_iota(jnp.int32, (192, TOK), 1)
    for which, target in ((core, keep), (1 - core, send)):
        for half in range(2):
            start = pl.multiple_of(half * 384 + which * 192, 192)
            block = attn[pl.ds(start, 192), :]
            block = jnp.where(token < scal[0], block, jnp.zeros_like(block))
            part = dot(block, cotangent, NN)
            for r in range(8):
                for c in range(2):
                    target[r * 2 + c, half] = part[r * 24 : r * 24 + 24, c * 384 : c * 384 + 384]
    out[...] = dot(wout[...].reshape(WIDTH, WIDTH), attn[...], NN).T


ANY = pl.BlockSpec(memory_space=pl.ANY)
VMEM = pl.BlockSpec(memory_space=pltpu.VMEM)
SMEM = pl.BlockSpec(memory_space=pltpu.SMEM)
PARAMS = pltpu.CompilerParams(vmem_limit_bytes=VMEM_BYTES)


def near_call(*operands, interpret=False):
    state = jax.ShapeDtypeStruct((TOK, TOK), F32)
    return pl.pallas_call(
        near_kernel,
        out_shape=(
            jax.ShapeDtypeStruct((HEADS, TOK, HEAD), BF),
            jax.ShapeDtypeStruct((WIDTH, TOK), F32),
            state,
            state,
        ),
        in_specs=[SMEM] + [ANY] * 7,
        out_specs=(VMEM,) * 4,
        scratch_shapes=[
            pltpu.VMEM((256, TILE), BF),
            pltpu.VMEM((4, 384, WIDTH), BF),
            pltpu.VMEM((4, 576, WIDTH), BF),
            pltpu.VMEM((256, WIDTH), BF),
            pltpu.VMEM((2 * WIDTH, 256), BF),
            pltpu.SemaphoreType.DMA((11,)),
        ],
        compiler_params=PARAMS,
        cost_estimate=pl.CostEstimate(
            flops=2_000_000_000, bytes_accessed=12_000_000, transcendentals=600_000
        ),
        interpret=interpret,
    )(*operands)


def far_call(*operands, interpret=False):
    part = jax.ShapeDtypeStruct((16, 2, 24, 384), F32)
    return pl.pallas_call(
        far_kernel,
        out_shape=(jax.ShapeDtypeStruct((TOK, WIDTH), F32), part, part),
        in_specs=[SMEM, ANY] + [VMEM] * 5 + [ANY] * 4,
        out_specs=(VMEM,) * 3,
        scratch_shapes=[
            pltpu.VMEM((16, 64, WIDTH), BF),
            pltpu.VMEM((4, 384, WIDTH), BF),
            pltpu.VMEM((4, 576, WIDTH), BF),
            pltpu.VMEM((4, 192, WIDTH), BF),
            pltpu.VMEM((FAR, WIDTH), BF),
            pltpu.VMEM((2 * WIDTH, FAR), BF),
            pltpu.VMEM((WIDTH, TOK), F32),
            pltpu.VMEM((WIDTH, TOK), BF),
            pltpu.SemaphoreType.DMA((13,)),
        ],
        compiler_params=PARAMS,
        cost_estimate=pl.CostEstimate(
            flops=3_000_000_000, bytes_accessed=16_000_000, transcendentals=1_000_000
        ),
        interpret=interpret,
    )(*operands)


def spread(block, axes, size):
    return lax.all_to_all(
        jnp.broadcast_to(block[None], (size,) + block.shape), axes, 0, 0, tiled=True
    )


def swap(value, axis):
    return lax.ppermute(value, axis, [(0, 1), (1, 0)])


def marked(rows, offsets, count):
    lane = lax.broadcasted_iota(jnp.int32, rows.shape, 1)
    mark = jnp.where(lane == 0, BF(MARK), BF(0))
    return jnp.where((offsets < count)[:, None], rows, mark)


def shards(tiles, counts, w_in, w_qkv, w_out, cotangent):
    rows = tiles[0]
    count = counts[0, 0]
    yx = lax.axis_index("y") * 4 + lax.axis_index("x")
    zh, core = lax.axis_index("zh"), lax.axis_index("core")
    own = jnp.concatenate([w_in, w_qkv.T, w_out.T], axis=0)
    piece = swap(lax.dynamic_slice(own, (yx * (PACK // 16), 0), (PACK // 16, WIDTH)), "zh")
    distant = marked(rows[0::DIL], jnp.arange(4) * DIL, count)
    line = spread(jnp.concatenate([distant[:, :WIDTH], distant[:, WIDTH:]], axis=0), "zl", 8)
    mate = swap(own, "core")
    even = rows[0::2]
    partner = lax.ppermute(
        marked(even, jnp.arange(TOK // 2) * 2, count), "zl", [(i, i ^ 1) for i in range(8)]
    )
    piece, line, mate, partner = lax.optimization_barrier((piece, line, mate, partner))
    got = spread(piece, YX, 16).reshape(PACK, WIDTH)
    far_rows = jnp.concatenate(
        [line[:, :4].reshape(32, WIDTH), line[:, 4:].reshape(32, WIDTH)], axis=0
    )
    far = spread(far_rows, YX, 16)
    cross = swap(got, "core")
    scal = jnp.stack([count, zh, core]).astype(jnp.int32)
    packs = (own, mate, got, cross)
    state = near_call(scal, rows, even, partner, *packs)
    out, keep, send = far_call(scal, far, *state, cotangent[0], *packs)
    pair = (keep + swap(send, "core")).astype(BF)
    plane = lax.all_to_all(pair, YX, 0, 0, tiled=True)
    plane = jnp.sum(plane.astype(F32), axis=0).astype(BF)
    column = jnp.broadcast_to(plane[:, None], (2, 8, 24, 384)).reshape(16, 24, 384)
    column = lax.all_to_all(column, ("zh", "zl"), 0, 0, tiled=True)
    total = jnp.sum(column.astype(F32), axis=0)
    whole = spread(total, YX, 16)
    grad = whole.reshape(8, 2, 24, 384).transpose(0, 2, 1, 3).reshape(192, WIDTH)
    return (out[None], grad)


def solution(mesh):
    fine = Mesh(mesh.devices.reshape(4, 4, 8, 2, 2), ("y", "x", "zl", "zh", "core"))
    seq, slide = ("y", "x", "zl"), ("zh", "core")
    placed = (
        P(slide, seq, None),
        P(slide, seq),
        P(slide, None),
        P(None, slide),
        P(None, slide),
        P(slide, seq, None),
    )
    return jax.shard_map(
        shards,
        mesh=fine,
        in_specs=placed,
        out_specs=(P(slide, seq, None), P(slide, None)),
        check_vma=False,
    )
```

```python
import jax
import jax.numpy as jnp
from jax import lax
from jax.experimental import pallas as pl
from jax.experimental.pallas import tpu as pltpu
from jax.sharding import Mesh
from jax.sharding import PartitionSpec as P

WIDTH = 768
TILE = 1536
HEADS = 16
HEAD = 48
DIL = 32
TOK = 128
FAR = 512
PACK = 1152
YX = ("y", "x")
ZL = ("zm", "zn")
NT = (((1,), (1,)), ((), ()))
NN = (((1,), (0,)), ((), ()))
BF = jnp.bfloat16
F32 = jnp.float32
MARK = 64.0
LOW = -1e30
LOG2 = 0.6931471805599453


def dot(a, b, dims):
    return lax.dot_general(a, b, dims, preferred_element_type=F32)


def weight_moves(scal, packs, win, wqkv):
    zh, core = scal[1], scal[2]
    places = (zh * 2 + core, zh * 2 + 1 - core, (1 - zh) * 2 + core, (1 - zh) * 2 + 1 - core)
    first = [(p.at[pl.ds(0, 384)], win.at[s]) for p, s in zip(packs, places)]
    second = [(p.at[pl.ds(384, 576)], wqkv.at[s]) for p, s in zip(packs, places)]
    return first, second


def key_bias(block):
    lane = lax.broadcasted_iota(jnp.int32, (16, TOK), 1)
    pick = jnp.where(lane == 0, F32(1), F32(0)).astype(BF)
    return jnp.where(dot(pick, block[:, :TOK], NT)[0:1] > MARK / 2, F32(LOW), F32(0))


def attend(query, kv, bias, mixed):
    column = lax.broadcasted_iota(jnp.int32, (TOK, TOK), 1)
    tops = jnp.zeros((TOK, TOK), F32)
    totals = jnp.ones((TOK, TOK), F32)
    for h in range(HEADS):
        s = dot(query(h), kv[pl.ds(h * HEAD, HEAD), :], NN) * F32(HEAD**-0.5) + bias
        top = jnp.max(s, axis=1, keepdims=True)
        p = jnp.exp(s - top)
        tops = jnp.where(column == h, top, tops)
        totals = jnp.where(column == h, jnp.sum(p, axis=1, keepdims=True), totals)
        mixed[pl.ds(h * HEAD, HEAD), :] = dot(
            kv[pl.ds(WIDTH + h * HEAD, HEAD), :], p.astype(BF), NT
        )
    return tops.T, totals.T


def near_kernel(
    scal, rows, partner, own, mate, got, cross, query, mixed, tops, totals, near, win, wqkv, hid, kv, sems
):
    first, second = weight_moves(scal, (own, mate, got, cross), win, wqkv)
    moves = [
        (rows, near.at[pl.ds(0, TOK)]),
        (partner, near.at[pl.ds(TOK, TOK // 2)]),
    ]
    moves = moves + first + second
    copies = [pltpu.make_async_copy(s, d, sems.at[i]) for i, (s, d) in enumerate(moves)]
    for c in copies:
        c.start()
    near[pl.ds(192, 64), :] = jnp.zeros((64, TILE), BF)
    for c in copies[:6]:
        c.wait()
    hid[...] = dot(near[...], win[...].reshape(TILE, WIDTH), NN).astype(BF)
    for c in copies[6:]:
        c.wait()
    flat = wqkv[...].reshape(3 * WIDTH, WIDTH)
    kv[...] = dot(flat[WIDTH:], hid[...], NT).astype(BF)
    own_hid = hid[pl.ds(0, TOK), :]
    for h in range(HEADS):
        query[h] = dot(own_hid, flat[h * HEAD : (h + 1) * HEAD], NT).astype(BF)
    lane = lax.broadcasted_iota(jnp.int32, (1, TOK), 1)
    twice = jnp.where(lane & 1 == 0, F32(LOG2), F32(0))
    bias = jnp.concatenate(
        [
            jnp.where(lane < scal[0], twice, F32(LOW)),
            key_bias(near[pl.ds(TOK, 64), :]),
            jnp.full((1, 64), LOW, F32),
        ],
        axis=1,
    )
    tops[...], totals[...] = attend(lambda h: query[h], kv, bias, mixed)


def far_kernel(
    scal,
    far,
    query,
    near_mixed,
    near_tops,
    near_totals,
    cot,
    own,
    mate,
    got,
    cross,
    over_rest,
    cross_rest,
    out,
    keep,
    send,
    win,
    wqkv,
    wout,
    hid,
    kv,
    mixed,
    attn,
    sems,
):
    zh, core = scal[1], scal[2]
    first, second = weight_moves(scal, (own, mate, got, cross), win, wqkv)
    places = (zh * 2 + core, zh * 2 + 1 - core, (1 - zh) * 2 + core, (1 - zh) * 2 + 1 - core)
    last = [(p.at[pl.ds(960, 192)], wout.at[s]) for p, s in zip((own, mate), places[:2])]
    for p, rest, s in zip((got, cross), (over_rest, cross_rest), places[2:]):
        last.append((p.at[pl.ds(960, 64)], wout.at[s, pl.ds(0, 64)]))
        last.append((rest, wout.at[s, pl.ds(64, 128)]))
    moves = first + second + last
    copies = [pltpu.make_async_copy(s, d, sems.at[i]) for i, (s, d) in enumerate(moves)]
    for c in copies:
        c.start()
    for c in copies[:4]:
        c.wait()
    left = far[:, pl.ds(0, 32), :].reshape(FAR, WIDTH)
    right = far[:, pl.ds(32, 32), :].reshape(FAR, WIDTH)
    weight = win[...].reshape(TILE, WIDTH)
    hid[...] = (dot(left, weight[:WIDTH], NN) + dot(right, weight[WIDTH:], NN)).astype(BF)
    for c in copies[4:8]:
        c.wait()
    kv[...] = dot(wqkv[...].reshape(3 * WIDTH, WIDTH)[WIDTH:], hid[...], NT).astype(BF)
    far_tops, far_totals = attend(lambda h: query[h], kv, key_bias(left), mixed)
    top = jnp.maximum(near_tops[...], far_tops)
    near_scale, far_scale = jnp.exp(near_tops[...] - top), jnp.exp(far_tops - top)
    inverse = 1.0 / (near_totals[...] * near_scale + far_totals * far_scale)
    near_scale, far_scale = near_scale * inverse, far_scale * inverse
    for h in range(HEADS):
        at = pl.ds(h * HEAD, HEAD)
        attn[at, :] = (
            near_mixed[at, :] * near_scale[h : h + 1, :] + mixed[at, :] * far_scale[h : h + 1, :]
        ).astype(BF)
    cotangent = cot[...]
    token = lax.broadcasted_iota(jnp.int32, (192, TOK), 1)
    for which, target in ((core, keep), (1 - core, send)):
        for half in range(2):
            start = pl.multiple_of(half * 384 + which * 192, 192)
            block = attn[pl.ds(start, 192), :]
            block = jnp.where(token < scal[0], block, jnp.zeros_like(block))
            part = dot(block, cotangent, NN)
            for r in range(8):
                for c in range(2):
                    target[r * 2 + c, half] = part[r * 24 : r * 24 + 24, c * 384 : c * 384 + 384].astype(
                        target.dtype
                    )
    for c in copies[8:]:
        c.wait()
    out[...] = dot(wout[...].reshape(WIDTH, WIDTH), attn[...], NN).T


ANY = pl.BlockSpec(memory_space=pl.ANY)
VMEM = pl.BlockSpec(memory_space=pltpu.VMEM)
SMEM = pl.BlockSpec(memory_space=pltpu.SMEM)


def room(mebibytes):
    return pltpu.CompilerParams(vmem_limit_bytes=mebibytes * 1024 * 1024)


def prepare_kernel(scal, rows, w_in, w_qkv, w_out, own, ahead, even, sixteen, sems):
    count, zh, at = scal[0], scal[1], scal[3]
    moves = [
        (w_in, own.at[pl.ds(0, 384)]),
        (w_qkv, own.at[pl.ds(384, 576)]),
        (w_out, own.at[pl.ds(960, 192)]),
    ]
    copies = [pltpu.make_async_copy(s, d, sems.at[i]) for i, (s, d) in enumerate(moves)]
    for c in copies:
        c.start()
    block = at // 16

    def fetch(source, first):
        start = pl.multiple_of((block - first) * 16, 16)
        copy = pltpu.make_async_copy(source.at[pl.ds(start, 16)], sixteen, sems.at[3])
        copy.start()
        copy.wait()

    @pl.when(block < 24)
    def _():
        fetch(w_in, 0)

    @pl.when((block >= 24) & (block < 60))
    def _():
        fetch(w_qkv, 24)

    @pl.when(block >= 60)
    def _():
        fetch(w_out, 60)

    wide = sixteen[...].astype(F32)
    eight = jnp.where(at - block * 16 > 0, wide[8:16], wide[0:8])
    lane = lax.broadcasted_iota(jnp.int32, (1, TILE), 1)
    mark = jnp.where(lane == 0, F32(MARK), F32(0))
    distant = jnp.concatenate(
        [
            jnp.where(DIL * j < count, rows[pl.ds(DIL * j, 16), :].astype(F32)[0:1], mark)
            for j in range(4)
        ],
        axis=0,
    )
    far = jnp.concatenate([distant[:, :WIDTH], distant[:, WIDTH:]], axis=0)
    for half in range(2):
        value = jnp.where(zh == half, far, eight)
        ahead[half] = jnp.concatenate([value] * 8, axis=0).astype(BF)
    row = lax.broadcasted_iota(jnp.int32, (TOK // 2, TOK), 0)
    source = lax.broadcasted_iota(jnp.int32, (TOK // 2, TOK), 1)
    pick = jnp.where((source == 2 * row) & (source < count), F32(1), F32(0)).astype(BF)
    marks = jnp.where(
        2 * lax.broadcasted_iota(jnp.int32, (TOK // 2, TILE), 0) < count, F32(0), mark
    )
    even[...] = (dot(pick, rows[...], NN) + marks).astype(BF)
    for c in copies:
        c.wait()


def prepare_call(*operands, interpret=False):
    return pl.pallas_call(
        prepare_kernel,
        out_shape=(
            jax.ShapeDtypeStruct((PACK, WIDTH), BF),
            jax.ShapeDtypeStruct((2, 64, WIDTH), BF),
            jax.ShapeDtypeStruct((TOK // 2, TILE), BF),
        ),
        in_specs=[SMEM, VMEM] + [ANY] * 3,
        out_specs=(ANY, VMEM, VMEM),
        scratch_shapes=[pltpu.VMEM((16, WIDTH), BF), pltpu.SemaphoreType.DMA((4,))],
        compiler_params=room(62),
        interpret=interpret,
    )(*operands)


def split_kernel(scal, line, pieces, rows):
    zh = scal[1]
    piece = line[1 - zh]
    target = lax.broadcasted_iota(jnp.int32, (64, 64), 0)
    source = lax.broadcasted_iota(jnp.int32, (64, 64), 1)
    origin = (target & 31) // 4 * 8 + target // 32 * 4 + (target & 3)
    pick = jnp.where(source == origin, F32(1), F32(0)).astype(BF)
    ordered = dot(pick, line[zh], NN).astype(BF)
    for i in range(16):
        pieces[i] = piece
        rows[i] = ordered


def split_call(*operands, interpret=False):
    payload = jax.ShapeDtypeStruct((16, 64, WIDTH), BF)
    return pl.pallas_call(
        split_kernel,
        out_shape=(payload, payload),
        in_specs=[SMEM, VMEM],
        out_specs=(VMEM, VMEM),
        compiler_params=room(16),
        interpret=interpret,
    )(*operands)


def near_call(*operands, interpret=False):
    state = jax.ShapeDtypeStruct((TOK, TOK), F32)
    return pl.pallas_call(
        near_kernel,
        out_shape=(
            jax.ShapeDtypeStruct((HEADS, TOK, HEAD), BF),
            jax.ShapeDtypeStruct((WIDTH, TOK), F32),
            state,
            state,
        ),
        in_specs=[SMEM] + [ANY] * 6,
        out_specs=(VMEM,) * 4,
        scratch_shapes=[
            pltpu.VMEM((256, TILE), BF),
            pltpu.VMEM((4, 384, WIDTH), BF),
            pltpu.VMEM((4, 576, WIDTH), BF),
            pltpu.VMEM((256, WIDTH), BF),
            pltpu.VMEM((2 * WIDTH, 256), BF),
            pltpu.SemaphoreType.DMA((10,)),
        ],
        compiler_params=room(62),
        cost_estimate=pl.CostEstimate(
            flops=2_000_000_000, bytes_accessed=12_000_000, transcendentals=600_000
        ),
        interpret=interpret,
    )(*operands)


def far_call(*operands, interpret=False):
    part = jax.ShapeDtypeStruct((16, 2, 24, 384), F32)
    sent = jax.ShapeDtypeStruct((16, 2, 24, 384), BF)
    return pl.pallas_call(
        far_kernel,
        out_shape=(jax.ShapeDtypeStruct((TOK, WIDTH), F32), part, sent),
        in_specs=[SMEM] + [VMEM] * 6 + [ANY] * 6,
        out_specs=(VMEM,) * 3,
        scratch_shapes=[
            pltpu.VMEM((4, 384, WIDTH), BF),
            pltpu.VMEM((4, 576, WIDTH), BF),
            pltpu.VMEM((4, 192, WIDTH), BF),
            pltpu.VMEM((FAR, WIDTH), BF),
            pltpu.VMEM((2 * WIDTH, FAR), BF),
            pltpu.VMEM((WIDTH, TOK), F32),
            pltpu.VMEM((WIDTH, TOK), BF),
            pltpu.SemaphoreType.DMA((14,)),
        ],
        compiler_params=room(60),
        cost_estimate=pl.CostEstimate(
            flops=3_000_000_000, bytes_accessed=16_000_000, transcendentals=1_000_000
        ),
        interpret=interpret,
    )(*operands)


def spread(block, axes, size):
    return lax.all_to_all(
        jnp.broadcast_to(block[None], (size,) + block.shape), axes, 0, 0, tiled=True
    )


def swap(value, axis):
    return lax.ppermute(value, axis, [(0, 1), (1, 0)])


def shards(tiles, counts, w_in, w_qkv, w_out, cotangent):
    rows = tiles[0]
    count = counts[0, 0]
    yx = lax.axis_index("y") * 4 + lax.axis_index("x")
    zl = lax.axis_index("zm") * 4 + lax.axis_index("zn")
    zh, core = lax.axis_index("zh"), lax.axis_index("core")
    w_out = w_out.T
    scal = jnp.stack([count, zh, core, yx * 64 + zl * 8]).astype(jnp.int32)
    own, ahead, even = prepare_call(scal, rows, w_in, w_qkv.T, w_out)
    line = lax.all_to_all(ahead.reshape(16, 8, WIDTH), ("zh",) + ZL, 0, 0, tiled=True)
    line = line.reshape(2, 64, WIDTH)
    mate = swap(own, "core")
    partner = lax.ppermute(even, "zn", [(i, i ^ 1) for i in range(4)])
    line, mate, partner = lax.optimization_barrier((line, mate, partner))
    pieces, far_rows = split_call(scal, line)
    got = lax.all_to_all(pieces, YX, 0, 0, tiled=True).reshape(1024, WIDTH)
    over_rest = swap(w_out[64:], "zh")
    got, over_rest, far_rows = lax.optimization_barrier((got, over_rest, far_rows))
    far = lax.all_to_all(far_rows, YX, 0, 0, tiled=True)
    cross, cross_rest = swap(got, "core"), swap(over_rest, "core")
    packs = (own, mate, got, cross)
    state = near_call(scal, rows, partner, *packs)
    out, keep, send = far_call(
        scal, far, *state, cotangent[0], *packs, over_rest, cross_rest
    )
    pair = (keep + swap(send, "core").astype(F32)).astype(BF)
    plane = lax.all_to_all(pair, YX, 0, 0, tiled=True)
    plane = jnp.sum(plane.astype(F32), axis=0).astype(BF)
    near_z = spread(plane, "zn", 4)
    near_z = jnp.sum(near_z.astype(F32), axis=0).astype(BF)
    column = jnp.broadcast_to(near_z[:, None], (2, 2, 24, 384)).reshape(4, 24, 384)
    column = lax.all_to_all(column, ("zh", "zm"), 0, 0, tiled=True)
    total = jnp.sum(column.astype(F32), axis=0)
    whole = spread(total, YX, 16)
    grad = whole.reshape(8, 2, 24, 384).transpose(0, 2, 1, 3).reshape(192, WIDTH)
    return (out[None], grad)


def solution(mesh):
    fine = Mesh(mesh.devices.reshape(4, 4, 2, 4, 2, 2), ("y", "x", "zm", "zn", "zh", "core"))
    seq, slide = YX + ZL, ("zh", "core")
    placed = (
        P(slide, seq, None),
        P(slide, seq),
        P(slide, None),
        P(None, slide),
        P(None, slide),
        P(slide, seq, None),
    )
    return jax.shard_map(
        shards,
        mesh=fine,
        in_specs=placed,
        out_specs=(P(slide, seq, None), P(slide, None)),
        check_vma=False,
    )
```

```python
import jax
import jax.numpy as jnp
from jax import lax
from jax.experimental import pallas as pl
from jax.experimental.pallas import tpu as pltpu
from jax.sharding import Mesh
from jax.sharding import PartitionSpec as P

WIDTH = 768
TILE = 1536
HEADS = 16
HEAD = 48
DIL = 32
TOK = 128
FAR = 512
PACK = 1152
YX = ("y", "x")
Z = ("zh", "zl")
NT = (((1,), (1,)), ((), ()))
NN = (((1,), (0,)), ((), ()))
BF = jnp.bfloat16
F32 = jnp.float32
MARK = 64.0
LOW = -1e30
LOG2 = 0.6931471805599453


def dot(a, b, dims):
    return lax.dot_general(a, b, dims, preferred_element_type=F32)


def key_bias(block):
    lane = lax.broadcasted_iota(jnp.int32, (16, TOK), 1)
    pick = jnp.where(lane == 0, F32(1), F32(0)).astype(BF)
    return jnp.where(dot(pick, block[:, :TOK], NT)[0:1] > MARK / 2, F32(LOW), F32(0))


def layer_kernel(
    scal,
    rows,
    partner,
    own,
    mate,
    got,
    cross,
    over_rest,
    cross_rest,
    cot,
    out,
    keep,
    send,
    near,
    far,
    win,
    wqkv,
    wout,
    hid,
    kv,
    mixed,
    attn,
    sems,
):
    count, zh, core = scal[0], scal[1], scal[2]
    mine, other = zh * 2 + core, zh * 2 + 1 - core
    over, over_other = (1 - zh) * 2 + core, (1 - zh) * 2 + 1 - core
    arrived = got.at[:, pl.ds(0, 64)]
    moves = [
        (own.at[pl.ds(0, 6)], win.at[mine]),
        (mate.at[pl.ds(0, 6)], win.at[other]),
        (arrived.at[pl.ds(0, 6)], win.at[over]),
        (cross.at[pl.ds(0, 6)], win.at[over_other]),
        (rows, near.at[pl.ds(0, TOK)]),
        (partner, near.at[pl.ds(TOK, TOK // 2)]),
        (got.at[:, pl.ds(64, 64)], far),
        (own.at[pl.ds(6, 9)], wqkv.at[mine]),
        (mate.at[pl.ds(6, 9)], wqkv.at[other]),
        (arrived.at[pl.ds(6, 9)], wqkv.at[over]),
        (cross.at[pl.ds(6, 9)], wqkv.at[over_other]),
        (own.at[pl.ds(15, 3)], wout.at[mine]),
        (mate.at[pl.ds(15, 3)], wout.at[other]),
        (arrived.at[15], wout.at[over, 0]),
        (cross.at[15], wout.at[over_other, 0]),
        (over_rest, wout.at[over, pl.ds(1, 2)]),
        (cross_rest, wout.at[over_other, pl.ds(1, 2)]),
    ]
    copies = [pltpu.make_async_copy(s, d, sems.at[i]) for i, (s, d) in enumerate(moves)]
    for c in copies:
        c.start()
    near[pl.ds(192, 64), :] = jnp.zeros((64, TILE), BF)
    lane = lax.broadcasted_iota(jnp.int32, (1, TOK), 1)
    twice = jnp.where(lane & 1 == 0, F32(LOG2), F32(0))
    for c in copies[:7]:
        c.wait()
    left = far[:, pl.ds(0, 32), :].reshape(FAR, WIDTH)
    right = far[:, pl.ds(32, 32), :].reshape(FAR, WIDTH)
    weight = win[...].reshape(TILE, WIDTH)
    hid[pl.ds(0, 256), :] = dot(near[...], weight, NN).astype(BF)
    hid[pl.ds(256, FAR), :] = (
        dot(left, weight[:WIDTH], NN) + dot(right, weight[WIDTH:], NN)
    ).astype(BF)
    bias = jnp.concatenate(
        [
            jnp.where(lane < count, twice, F32(LOW)),
            key_bias(near[pl.ds(TOK, 64), :]),
            jnp.full((1, 64), LOW, F32),
            key_bias(left),
        ],
        axis=1,
    )
    for c in copies[7:11]:
        c.wait()
    flat = wqkv[...].reshape(3 * WIDTH, WIDTH)
    kv[...] = dot(flat[WIDTH:], hid[...], NT).astype(BF)
    own_hid = hid[pl.ds(0, TOK), :]
    column = lax.broadcasted_iota(jnp.int32, (TOK, TOK), 1)
    totals = jnp.ones((TOK, TOK), F32)
    for h in range(HEADS):
        q = dot(own_hid, flat[h * HEAD : (h + 1) * HEAD], NT).astype(BF)
        s = dot(q, kv[pl.ds(h * HEAD, HEAD), :], NN) * F32(HEAD**-0.5) + bias
        p = jnp.exp(s - jnp.max(s, axis=1, keepdims=True))
        totals = jnp.where(column == h, jnp.sum(p, axis=1, keepdims=True), totals)
        mixed[pl.ds(h * HEAD, HEAD), :] = dot(
            kv[pl.ds(WIDTH + h * HEAD, HEAD), :], p.astype(BF), NT
        )
    inverse = 1.0 / totals.T
    for h in range(HEADS):
        at = pl.ds(h * HEAD, HEAD)
        attn[at, :] = (mixed[at, :] * inverse[h : h + 1, :]).astype(BF)
    cotangent = cot[...]
    token = lax.broadcasted_iota(jnp.int32, (192, TOK), 1)
    for which, target in ((core, keep), (1 - core, send)):
        for half in range(2):
            start = pl.multiple_of(half * 384 + which * 192, 192)
            block = attn[pl.ds(start, 192), :]
            block = jnp.where(token < count, block, jnp.zeros_like(block))
            part = dot(block, cotangent, NN)
            for r in range(8):
                for c in range(2):
                    target[r * 2 + c, half] = part[r * 24 : r * 24 + 24, c * 384 : c * 384 + 384].astype(
                        target.dtype
                    )
    for c in copies[11:]:
        c.wait()
    out[...] = dot(wout[...].reshape(WIDTH, WIDTH), attn[...], NN).T


ANY = pl.BlockSpec(memory_space=pl.ANY)
VMEM = pl.BlockSpec(memory_space=pltpu.VMEM)
SMEM = pl.BlockSpec(memory_space=pltpu.SMEM)


def room(mebibytes):
    return pltpu.CompilerParams(vmem_limit_bytes=mebibytes * 1024 * 1024)


def prepare_kernel(scal, rows, w_in, w_qkv, w_out, own, ahead, even, sems):
    count, zh, at = scal[0], scal[1], scal[3]
    moves = [
        (w_in, own.at[pl.ds(0, 384)]),
        (w_qkv, own.at[pl.ds(384, 576)]),
        (w_out, own.at[pl.ds(960, 192)]),
    ]
    copies = [pltpu.make_async_copy(s, d, sems.at[i]) for i, (s, d) in enumerate(moves)]
    for c in copies:
        c.start()
    lane = lax.broadcasted_iota(jnp.int32, (1, TILE), 1)
    mark = jnp.where(lane == 0, F32(MARK), F32(0))
    distant = jnp.concatenate(
        [
            jnp.where(DIL * j < count, rows[pl.ds(DIL * j, 16), :].astype(F32)[0:1], mark)
            for j in range(4)
        ],
        axis=0,
    )
    row = lax.broadcasted_iota(jnp.int32, (TOK // 2, TOK), 0)
    source = lax.broadcasted_iota(jnp.int32, (TOK // 2, TOK), 1)
    pick = jnp.where((source == 2 * row) & (source < count), F32(1), F32(0)).astype(BF)
    marks = jnp.where(
        2 * lax.broadcasted_iota(jnp.int32, (TOK // 2, TILE), 0) < count, F32(0), mark
    )
    even[...] = (dot(pick, rows[...], NN) + marks).astype(BF)
    for c in copies:
        c.wait()
    start = pl.multiple_of(at // 16 * 16, 16)
    wide = own[pl.ds(start, 16), :].astype(F32)
    eight = jnp.where(at > start, wide[8:16], wide[0:8])
    far = jnp.concatenate([distant[:, :WIDTH], distant[:, WIDTH:]], axis=0)
    for half in range(2):
        value = jnp.where(zh == half, far, eight)
        ahead[half] = jnp.concatenate([value] * 8, axis=0).astype(BF)


def prepare_call(*operands, interpret=False):
    return pl.pallas_call(
        prepare_kernel,
        out_shape=(
            jax.ShapeDtypeStruct((PACK, WIDTH), BF),
            jax.ShapeDtypeStruct((2, 64, WIDTH), BF),
            jax.ShapeDtypeStruct((TOK // 2, TILE), BF),
        ),
        in_specs=[SMEM, VMEM] + [ANY] * 3,
        out_specs=(VMEM, VMEM, VMEM),
        scratch_shapes=[pltpu.SemaphoreType.DMA((3,))],
        compiler_params=room(62),
        interpret=interpret,
    )(*operands)


def split_kernel(scal, line, payload):
    zh = scal[1]
    piece = line[1 - zh]
    target = lax.broadcasted_iota(jnp.int32, (64, 64), 0)
    source = lax.broadcasted_iota(jnp.int32, (64, 64), 1)
    origin = (target & 31) // 4 * 8 + target // 32 * 4 + (target & 3)
    pick = jnp.where(source == origin, F32(1), F32(0)).astype(BF)
    ordered = dot(pick, line[zh], NN).astype(BF)
    both = jnp.concatenate([piece, ordered], axis=0)
    for i in range(16):
        payload[i] = both


def split_call(*operands, interpret=False):
    return pl.pallas_call(
        split_kernel,
        out_shape=jax.ShapeDtypeStruct((16, 128, WIDTH), BF),
        in_specs=[SMEM, VMEM],
        out_specs=VMEM,
        compiler_params=room(16),
        interpret=interpret,
    )(*operands)


def layer_call(*operands, interpret=False):
    part = jax.ShapeDtypeStruct((16, 2, 24, 384), F32)
    sent = jax.ShapeDtypeStruct((16, 2, 24, 384), BF)
    return pl.pallas_call(
        layer_kernel,
        out_shape=(jax.ShapeDtypeStruct((TOK, WIDTH), F32), part, sent),
        in_specs=[SMEM] + [ANY] * 8 + [VMEM],
        out_specs=(VMEM,) * 3,
        scratch_shapes=[
            pltpu.VMEM((256, TILE), BF),
            pltpu.VMEM((16, 64, WIDTH), BF),
            pltpu.VMEM((4, 6, 64, WIDTH), BF),
            pltpu.VMEM((4, 9, 64, WIDTH), BF),
            pltpu.VMEM((4, 3, 64, WIDTH), BF),
            pltpu.VMEM((WIDTH, WIDTH), BF),
            pltpu.VMEM((2 * WIDTH, WIDTH), BF),
            pltpu.VMEM((WIDTH, TOK), F32),
            pltpu.VMEM((WIDTH, TOK), BF),
            pltpu.SemaphoreType.DMA((17,)),
        ],
        compiler_params=room(62),
        interpret=interpret,
    )(*operands)


def spread(block, axes, size):
    return lax.all_to_all(
        jnp.broadcast_to(block[None], (size,) + block.shape), axes, 0, 0, tiled=True
    )


def swap(value, axis):
    return lax.ppermute(value, axis, [(0, 1), (1, 0)])


def shards(tiles, counts, w_in, w_qkv, w_out, cotangent):
    rows = tiles[0]
    count = counts[0, 0]
    yx = lax.axis_index("y") * 4 + lax.axis_index("x")
    zl = lax.axis_index("zl")
    zh, core = lax.axis_index("zh"), lax.axis_index("core")
    w_out = w_out.T
    scal = jnp.stack([count, zh, core, yx * 64 + zl * 8]).astype(jnp.int32)
    own, ahead, even = prepare_call(scal, rows, w_in, w_qkv.T, w_out)
    line = lax.all_to_all(ahead.reshape(16, 8, WIDTH), Z, 0, 0, tiled=True)
    mate = swap(own, "core")
    line, mate, even = lax.optimization_barrier((line.reshape(2, 64, WIDTH), mate, even))
    partner = lax.ppermute(even, "zl", [(i, i ^ 1) for i in range(8)])
    over_rest = swap(w_out[64:], "zh")
    got = lax.all_to_all(split_call(scal, line), YX, 0, 0, tiled=True)
    cross_rest = swap(over_rest, "core")
    got, over_rest, cross_rest, partner = lax.optimization_barrier(
        (got, over_rest, cross_rest, partner)
    )
    cross = swap(got[:, :64], "core")
    out, keep, send = layer_call(
        scal,
        rows,
        partner,
        own.reshape(18, 64, WIDTH),
        mate.reshape(18, 64, WIDTH),
        got,
        cross,
        over_rest.reshape(2, 64, WIDTH),
        cross_rest.reshape(2, 64, WIDTH),
        cotangent[0],
    )
    pair = (keep + swap(send, "core").astype(F32)).astype(BF)
    plane = lax.all_to_all(pair, YX, 0, 0, tiled=True)
    plane = jnp.sum(plane.astype(F32), axis=0).astype(BF)
    column = jnp.broadcast_to(plane[:, None], (2, 8, 24, 384)).reshape(16, 24, 384)
    column = lax.all_to_all(column, Z, 0, 0, tiled=True)
    total = jnp.sum(column.astype(F32), axis=0)
    whole = spread(total, YX, 16)
    grad = whole.reshape(8, 2, 24, 384).transpose(0, 2, 1, 3).reshape(192, WIDTH)
    return (out[None], grad)


def solution(mesh):
    fine = Mesh(mesh.devices.reshape(4, 4, 8, 2, 2), ("y", "x", "zl", "zh", "core"))
    seq, slide = YX + ("zl",), ("zh", "core")
    placed = (
        P(slide, seq, None),
        P(slide, seq),
        P(slide, None),
        P(None, slide),
        P(None, slide),
        P(slide, seq, None),
    )
    return jax.shard_map(
        shards,
        mesh=fine,
        in_specs=placed,
        out_specs=(P(slide, seq, None), P(slide, None)),
        check_vma=False,
    )
```

```python
import jax
import jax.numpy as jnp
from jax import lax
from jax.experimental import pallas as pl
from jax.experimental.pallas import tpu as pltpu
from jax.sharding import Mesh
from jax.sharding import PartitionSpec as P

WIDTH = 768
TILE = 1536
HEADS = 16
HEAD = 48
DIL = 32
TOK = 128
FAR = 512
PACK = 1152
YX = ("y", "x")
Z = ("zh", "zl")
NT = (((1,), (1,)), ((), ()))
NN = (((1,), (0,)), ((), ()))
BF = jnp.bfloat16
F32 = jnp.float32
MARK = 64.0
LOW = -1e30
SCALE = HEAD**-0.5 / 0.6931471805599453


def dot(a, b, dims):
    return lax.dot_general(a, b, dims, preferred_element_type=F32)


def key_bias(block):
    lane = lax.broadcasted_iota(jnp.int32, (16, TOK), 1)
    pick = jnp.where(lane == 0, F32(1), F32(0)).astype(BF)
    return jnp.where(dot(pick, block[:, :TOK], NT)[0:1] > MARK / 2, F32(LOW), F32(0))


def layer_kernel(
    scal,
    rows,
    partner,
    own,
    mate,
    got,
    cross,
    over_rest,
    cross_rest,
    cot,
    out,
    keep,
    send,
    given,
    win,
    wqkv,
    wout,
    hid,
    kv,
    attn,
    sems,
):
    count, zh, core = scal[0], scal[1], scal[2]
    mine, other = zh * 2 + core, zh * 2 + 1 - core
    over, over_other = (1 - zh) * 2 + core, (1 - zh) * 2 + 1 - core
    arrived = got.at[:, pl.ds(0, 64)]
    moves = [
        (own.at[pl.ds(0, 6)], win.at[mine]),
        (mate.at[pl.ds(0, 6)], win.at[other]),
        (arrived.at[pl.ds(0, 6)], win.at[over]),
        (cross.at[pl.ds(0, 6)], win.at[over_other]),
        (rows, given.at[pl.ds(0, 4)]),
        (partner, given.at[pl.ds(4, 2)]),
        (got.at[:, pl.ds(64, 32)], given.at[pl.ds(8, 16), :, pl.ds(0, WIDTH)]),
        (got.at[:, pl.ds(96, 32)], given.at[pl.ds(8, 16), :, pl.ds(WIDTH, WIDTH)]),
        (own.at[pl.ds(6, 9)], wqkv.at[mine]),
        (mate.at[pl.ds(6, 9)], wqkv.at[other]),
        (arrived.at[pl.ds(6, 9)], wqkv.at[over]),
        (cross.at[pl.ds(6, 9)], wqkv.at[over_other]),
        (own.at[pl.ds(15, 3)], wout.at[mine]),
        (mate.at[pl.ds(15, 3)], wout.at[other]),
        (arrived.at[15], wout.at[over, 0]),
        (cross.at[15], wout.at[over_other, 0]),
        (over_rest, wout.at[over, pl.ds(1, 2)]),
        (cross_rest, wout.at[over_other, pl.ds(1, 2)]),
    ]
    copies = [pltpu.make_async_copy(s, d, sems.at[i]) for i, (s, d) in enumerate(moves)]
    for c in copies:
        c.start()
    given[pl.ds(6, 2)] = jnp.zeros((2, 32, TILE), BF)
    lane = lax.broadcasted_iota(jnp.int32, (1, TOK), 1)
    twice = jnp.where(lane & 1 == 0, F32(1), F32(0))
    for c in copies[:8]:
        c.wait()
    keys = given[...].reshape(WIDTH, TILE)
    hid[...] = dot(keys, win[...].reshape(TILE, WIDTH), NN).astype(BF)
    bias = jnp.concatenate(
        [
            jnp.where(lane < count, twice, F32(LOW)),
            key_bias(keys[TOK : TOK + 64]),
            jnp.full((1, 64), LOW, F32),
            key_bias(keys[256:]),
        ],
        axis=1,
    )
    for c in copies[8:12]:
        c.wait()
    flat = wqkv[...].reshape(3 * WIDTH, WIDTH)
    kv[...] = dot(flat[WIDTH:], hid[...], NT).astype(BF)
    own_hid = hid[pl.ds(0, TOK), :]
    for h in range(HEADS):
        q = dot(own_hid, flat[h * HEAD : (h + 1) * HEAD], NT).astype(BF)
        s = dot(q, kv[pl.ds(h * HEAD, HEAD), :], NN) * F32(SCALE) + bias
        p = jnp.exp2(s - jnp.max(s, axis=1, keepdims=True))
        o = dot(p.astype(BF), kv[pl.ds(WIDTH + h * HEAD, HEAD), :], NT)
        o = o / jnp.sum(p, axis=1, keepdims=True)
        attn[pl.ds(h * HEAD, HEAD), :] = o.T.astype(BF)
    cotangent = cot[...]
    token = lax.broadcasted_iota(jnp.int32, (192, TOK), 1)
    for which, target in ((core, keep), (1 - core, send)):
        for half in range(2):
            start = pl.multiple_of(half * 384 + which * 192, 192)
            block = attn[pl.ds(start, 192), :]
            block = jnp.where(token < count, block, jnp.zeros_like(block))
            part = dot(block, cotangent, NN)
            for r in range(8):
                for c in range(2):
                    target[r * 2 + c, half] = part[r * 24 : r * 24 + 24, c * 384 : c * 384 + 384].astype(
                        target.dtype
                    )
    for c in copies[12:]:
        c.wait()
    out[...] = dot(wout[...].reshape(WIDTH, WIDTH), attn[...], NN).T


ANY = pl.BlockSpec(memory_space=pl.ANY)
VMEM = pl.BlockSpec(memory_space=pltpu.VMEM)
SMEM = pl.BlockSpec(memory_space=pltpu.SMEM)


def room(mebibytes):
    return pltpu.CompilerParams(vmem_limit_bytes=mebibytes * 1024 * 1024)


def prepare_kernel(scal, rows, w_in, w_qkv, w_out, own, ahead, even, tail, sems):
    count, zh, at = scal[0], scal[1], scal[3]
    moves = [
        (w_in, own.at[pl.ds(0, 384)]),
        (w_qkv, own.at[pl.ds(384, 576)]),
        (w_out, own.at[pl.ds(960, 192)]),
    ]
    copies = [pltpu.make_async_copy(s, d, sems.at[i]) for i, (s, d) in enumerate(moves)]
    for c in copies:
        c.start()
    lane = lax.broadcasted_iota(jnp.int32, (1, TILE), 1)
    mark = jnp.where(lane == 0, F32(MARK), F32(0))
    distant = jnp.concatenate(
        [
            jnp.where(DIL * j < count, rows[pl.ds(DIL * j, 16), :].astype(F32)[0:1], mark)
            for j in range(4)
        ],
        axis=0,
    )
    row = lax.broadcasted_iota(jnp.int32, (TOK // 2, TOK), 0)
    source = lax.broadcasted_iota(jnp.int32, (TOK // 2, TOK), 1)
    pick = jnp.where((source == 2 * row) & (source < count), F32(1), F32(0)).astype(BF)
    marks = jnp.where(
        2 * lax.broadcasted_iota(jnp.int32, (TOK // 2, TILE), 0) < count, F32(0), mark
    )
    even[...] = (dot(pick, rows[...], NN) + marks).astype(BF)
    for c in copies:
        c.wait()
    start = pl.multiple_of(at // 16 * 16, 16)
    wide = own[pl.ds(start, 16), :].astype(F32)
    eight = jnp.where(at > start, wide[8:16], wide[0:8])
    first = 8 * (at // 64)
    start = pl.multiple_of(1024 + first // 16 * 16, 16)
    wide = own[pl.ds(start, 16), :].astype(F32)
    last = jnp.where(first % 16 > 0, wide[8:16], wide[0:8])
    tail[...] = jnp.concatenate([last, last], axis=0).astype(BF)
    far = jnp.concatenate([distant[:, :WIDTH], distant[:, WIDTH:]], axis=0)
    for half in range(2):
        value = jnp.where(zh == half, far, eight)
        ahead[half] = jnp.concatenate([value] * 8, axis=0).astype(BF)


def prepare_call(*operands, interpret=False):
    return pl.pallas_call(
        prepare_kernel,
        out_shape=(
            jax.ShapeDtypeStruct((PACK, WIDTH), BF),
            jax.ShapeDtypeStruct((2, 64, WIDTH), BF),
            jax.ShapeDtypeStruct((TOK // 2, TILE), BF),
            jax.ShapeDtypeStruct((16, WIDTH), BF),
        ),
        in_specs=[SMEM, VMEM] + [ANY] * 3,
        out_specs=(VMEM,) * 4,
        scratch_shapes=[pltpu.SemaphoreType.DMA((3,))],
        compiler_params=room(62),
        interpret=interpret,
    )(*operands)


def split_kernel(scal, line, tail, payload):
    zh = scal[1]
    piece = line[1 - zh]
    target = lax.broadcasted_iota(jnp.int32, (64, 64), 0)
    source = lax.broadcasted_iota(jnp.int32, (64, 64), 1)
    origin = (target & 31) // 4 * 8 + target // 32 * 4 + (target & 3)
    pick = jnp.where(source == origin, F32(1), F32(0)).astype(BF)
    ordered = dot(pick, line[zh], NN).astype(BF)
    both = jnp.concatenate(
        [piece.astype(F32), ordered.astype(F32), tail[...].astype(F32)[0:8]], axis=0
    ).astype(BF)
    for i in range(16):
        payload[i] = both


def split_call(*operands, interpret=False):
    return pl.pallas_call(
        split_kernel,
        out_shape=jax.ShapeDtypeStruct((16, 136, WIDTH), BF),
        in_specs=[SMEM, VMEM, VMEM],
        out_specs=VMEM,
        compiler_params=room(16),
        interpret=interpret,
    )(*operands)


def layer_call(*operands, interpret=False):
    part = jax.ShapeDtypeStruct((16, 2, 24, 384), F32)
    sent = jax.ShapeDtypeStruct((16, 2, 24, 384), BF)
    return pl.pallas_call(
        layer_kernel,
        out_shape=(jax.ShapeDtypeStruct((TOK, WIDTH), F32), part, sent),
        in_specs=[SMEM] + [ANY] * 8 + [VMEM],
        out_specs=(VMEM,) * 3,
        scratch_shapes=[
            pltpu.VMEM((24, 32, TILE), BF),
            pltpu.VMEM((4, 6, 64, WIDTH), BF),
            pltpu.VMEM((4, 9, 64, WIDTH), BF),
            pltpu.VMEM((4, 3, 64, WIDTH), BF),
            pltpu.VMEM((WIDTH, WIDTH), BF),
            pltpu.VMEM((2 * WIDTH, WIDTH), BF),
            pltpu.VMEM((WIDTH, TOK), BF),
            pltpu.SemaphoreType.DMA((18,)),
        ],
        compiler_params=room(62),
        interpret=interpret,
    )(*operands)


def spread(block, axes, size):
    return lax.all_to_all(
        jnp.broadcast_to(block[None], (size,) + block.shape), axes, 0, 0, tiled=True
    )


def swap(value, axis):
    return lax.ppermute(value, axis, [(0, 1), (1, 0)])


def shards(tiles, counts, w_in, w_qkv, w_out, cotangent):
    rows = tiles[0]
    count = counts[0, 0]
    yx = lax.axis_index("y") * 4 + lax.axis_index("x")
    zl = lax.axis_index("zl")
    zh, core = lax.axis_index("zh"), lax.axis_index("core")
    w_out = w_out.T
    scal = jnp.stack([count, zh, core, yx * 64 + zl * 8]).astype(jnp.int32)
    own, ahead, even, tail = prepare_call(scal, rows, w_in, w_qkv.T, w_out)
    line = lax.all_to_all(ahead.reshape(16, 8, WIDTH), Z, 0, 0, tiled=True)
    mate = swap(own, "core")
    tail = swap(tail, "zh")
    partner = lax.ppermute(even, "zl", [(i, i ^ 1) for i in range(8)])
    line, mate, tail, partner = lax.optimization_barrier(
        (line.reshape(2, 64, WIDTH), mate, tail, partner)
    )
    got = lax.all_to_all(split_call(scal, line, tail), YX, 0, 0, tiled=True)
    over_rest = got[:, 128:].reshape(128, WIDTH)
    cross, cross_rest = swap(got[:, :64], "core"), swap(over_rest, "core")
    out, keep, send = layer_call(
        scal,
        rows.reshape(4, 32, TILE),
        partner.reshape(2, 32, TILE),
        own.reshape(18, 64, WIDTH),
        mate.reshape(18, 64, WIDTH),
        got,
        cross,
        over_rest.reshape(2, 64, WIDTH),
        cross_rest.reshape(2, 64, WIDTH),
        cotangent[0],
    )
    pair = (keep + swap(send, "core").astype(F32)).astype(BF)
    plane = lax.all_to_all(pair, YX, 0, 0, tiled=True)
    plane = jnp.sum(plane.astype(F32), axis=0).astype(BF)
    column = jnp.broadcast_to(plane[:, None], (2, 8, 24, 384)).reshape(16, 24, 384)
    column = lax.all_to_all(column, Z, 0, 0, tiled=True)
    total = jnp.sum(column.astype(F32), axis=0)
    whole = spread(total.astype(BF), YX, 16).astype(F32)
    grad = whole.reshape(8, 2, 24, 384).transpose(0, 2, 1, 3).reshape(192, WIDTH)
    return (out[None], grad)


def solution(mesh):
    fine = Mesh(mesh.devices.reshape(4, 4, 8, 2, 2), ("y", "x", "zl", "zh", "core"))
    seq, slide = YX + ("zl",), ("zh", "core")
    placed = (
        P(slide, seq, None),
        P(slide, seq),
        P(slide, None),
        P(None, slide),
        P(None, slide),
        P(slide, seq, None),
    )
    return jax.shard_map(
        shards,
        mesh=fine,
        in_specs=placed,
        out_specs=(P(slide, seq, None), P(slide, None)),
        check_vma=False,
    )
```

```python
import jax
import jax.numpy as jnp
from jax import lax
from jax.experimental import pallas as pl
from jax.experimental.pallas import tpu as pltpu
from jax.sharding import Mesh
from jax.sharding import PartitionSpec as P

WIDTH = 768
TILE = 1536
HEADS = 16
HEAD = 48
DIL = 32
TOK = 128
FAR = 512
PACK = 1152
YX = ("y", "x")
Z = ("zh", "zl")
NT = (((1,), (1,)), ((), ()))
NN = (((1,), (0,)), ((), ()))
BF = jnp.bfloat16
F32 = jnp.float32
MARK = 64.0
LOW = -1e30
SCALE = HEAD**-0.5 / 0.6931471805599453


def dot(a, b, dims):
    return lax.dot_general(a, b, dims, preferred_element_type=F32)


def key_bias(block):
    lane = lax.broadcasted_iota(jnp.int32, (16, TOK), 1)
    pick = jnp.where(lane == 0, F32(1), F32(0)).astype(BF)
    return jnp.where(dot(pick, block[:, :TOK], NT)[0:1] > MARK / 2, F32(LOW), F32(0))


def layer_kernel(
    scal,
    rows,
    partner,
    own,
    mate,
    got,
    cross,
    over_rest,
    cross_rest,
    cot,
    out,
    keep,
    send,
    given,
    win,
    wqkv,
    wout,
    hid,
    kv,
    attn,
    sems,
):
    count, zh, core = scal[0], scal[1], scal[2]
    mine, other = zh * 2 + core, zh * 2 + 1 - core
    over, over_other = (1 - zh) * 2 + core, (1 - zh) * 2 + 1 - core
    arrived = got.at[:, pl.ds(0, 64)]
    moves = [
        (own.at[pl.ds(0, 6)], win.at[mine]),
        (mate.at[pl.ds(0, 6)], win.at[other]),
        (arrived.at[pl.ds(0, 6)], win.at[over]),
        (cross.at[pl.ds(0, 6)], win.at[over_other]),
        (rows, given.at[pl.ds(0, 4)]),
        (partner, given.at[pl.ds(4, 2)]),
        (got.at[:, pl.ds(64, 32)], given.at[pl.ds(8, 16), :, pl.ds(0, WIDTH)]),
        (got.at[:, pl.ds(96, 32)], given.at[pl.ds(8, 16), :, pl.ds(WIDTH, WIDTH)]),
        (own.at[pl.ds(6, 9)], wqkv.at[mine]),
        (mate.at[pl.ds(6, 9)], wqkv.at[other]),
        (arrived.at[pl.ds(6, 9)], wqkv.at[over]),
        (cross.at[pl.ds(6, 9)], wqkv.at[over_other]),
        (own.at[pl.ds(15, 3)], wout.at[mine]),
        (mate.at[pl.ds(15, 3)], wout.at[other]),
        (arrived.at[15], wout.at[over, 0]),
        (cross.at[15], wout.at[over_other, 0]),
        (over_rest, wout.at[over, pl.ds(1, 2)]),
        (cross_rest, wout.at[over_other, pl.ds(1, 2)]),
    ]
    copies = [pltpu.make_async_copy(s, d, sems.at[i]) for i, (s, d) in enumerate(moves)]
    for c in copies:
        c.start()
    given[pl.ds(6, 2)] = jnp.zeros((2, 32, TILE), BF)
    lane = lax.broadcasted_iota(jnp.int32, (1, TOK), 1)
    twice = jnp.where(lane & 1 == 0, F32(1), F32(0))
    for c in copies[:8]:
        c.wait()
    keys = given[...].reshape(WIDTH, TILE)
    hid[...] = dot(keys, win[...].reshape(TILE, WIDTH), NN).astype(BF)
    bias = jnp.concatenate(
        [
            jnp.where(lane < count, twice, F32(LOW)),
            key_bias(keys[TOK : TOK + 64]),
            jnp.full((1, 64), LOW, F32),
            key_bias(keys[256:]),
        ],
        axis=1,
    )
    for c in copies[8:12]:
        c.wait()
    flat = wqkv[...].reshape(3 * WIDTH, WIDTH)
    kv[...] = dot(flat[WIDTH:], hid[...], NT).astype(BF)
    own_hid = hid[pl.ds(0, TOK), :]
    for h in range(HEADS):
        q = dot(own_hid, flat[h * HEAD : (h + 1) * HEAD], NT).astype(BF)
        s = dot(q, kv[pl.ds(h * HEAD, HEAD), :], NN) * F32(SCALE) + bias
        p = jnp.exp2(s - jnp.max(s, axis=1, keepdims=True))
        o = dot(p.astype(BF), kv[pl.ds(WIDTH + h * HEAD, HEAD), :], NT)
        o = o / jnp.sum(p, axis=1, keepdims=True)
        attn[pl.ds(h * HEAD, HEAD), :] = o.T.astype(BF)
    cotangent = cot[...]
    token = lax.broadcasted_iota(jnp.int32, (192, TOK), 1)
    for which, target in ((core, keep), (1 - core, send)):
        for half in range(2):
            start = pl.multiple_of(half * 384 + which * 192, 192)
            block = attn[pl.ds(start, 192), :]
            block = jnp.where(token < count, block, jnp.zeros_like(block))
            part = dot(block, cotangent, NN)
            for r in range(8):
                for c in range(2):
                    target[r * 2 + c, half] = part[r * 24 : r * 24 + 24, c * 384 : c * 384 + 384].astype(
                        target.dtype
                    )
    for c in copies[12:]:
        c.wait()
    out[...] = dot(wout[...].reshape(WIDTH, WIDTH), attn[...], NN).T


ANY = pl.BlockSpec(memory_space=pl.ANY)
VMEM = pl.BlockSpec(memory_space=pltpu.VMEM)
SMEM = pl.BlockSpec(memory_space=pltpu.SMEM)


def room(mebibytes):
    return pltpu.CompilerParams(vmem_limit_bytes=mebibytes * 1024 * 1024)


def prepare_kernel(scal, rows, w_in, w_qkv, w_out, own, ahead, even, sems):
    count, zh, at = scal[0], scal[1], scal[3]
    moves = [
        (w_in, own.at[pl.ds(0, 384)]),
        (w_qkv, own.at[pl.ds(384, 576)]),
        (w_out, own.at[pl.ds(960, 192)]),
    ]
    copies = [pltpu.make_async_copy(s, d, sems.at[i]) for i, (s, d) in enumerate(moves)]
    for c in copies:
        c.start()
    lane = lax.broadcasted_iota(jnp.int32, (1, TILE), 1)
    mark = jnp.where(lane == 0, F32(MARK), F32(0))
    distant = jnp.concatenate(
        [
            jnp.where(DIL * j < count, rows[pl.ds(DIL * j, 16), :].astype(F32)[0:1], mark)
            for j in range(4)
        ],
        axis=0,
    )
    row = lax.broadcasted_iota(jnp.int32, (TOK // 2, TOK), 0)
    source = lax.broadcasted_iota(jnp.int32, (TOK // 2, TOK), 1)
    pick = jnp.where((source == 2 * row) & (source < count), F32(1), F32(0)).astype(BF)
    marks = jnp.where(
        2 * lax.broadcasted_iota(jnp.int32, (TOK // 2, TILE), 0) < count, F32(0), mark
    )
    even[...] = (dot(pick, rows[...], NN) + marks).astype(BF)
    for c in copies:
        c.wait()
    start = pl.multiple_of(at // 16 * 16, 16)
    wide = own[pl.ds(start, 16), :].astype(F32)
    eight = jnp.where(at > start, wide[8:16], wide[0:8])
    first = 8 * (at // 64)
    start = pl.multiple_of(1024 + first // 16 * 16, 16)
    wide = own[pl.ds(start, 16), :].astype(F32)
    last = jnp.where(first % 16 > 0, wide[8:16], wide[0:8])
    sent = jnp.concatenate([eight, last], axis=0)
    far = jnp.concatenate([distant[:, :WIDTH], distant[:, WIDTH:], jnp.zeros((8, WIDTH), F32)], axis=0)
    for half in range(2):
        value = jnp.where(zh == half, far, sent)
        ahead[half] = jnp.concatenate([value] * 8, axis=0).astype(BF)


def prepare_call(*operands, interpret=False):
    return pl.pallas_call(
        prepare_kernel,
        out_shape=(
            jax.ShapeDtypeStruct((PACK, WIDTH), BF),
            jax.ShapeDtypeStruct((2, 128, WIDTH), BF),
            jax.ShapeDtypeStruct((TOK // 2, TILE), BF),
        ),
        in_specs=[SMEM, VMEM] + [ANY] * 3,
        out_specs=(VMEM,) * 3,
        scratch_shapes=[pltpu.SemaphoreType.DMA((3,))],
        compiler_params=room(62),
        interpret=interpret,
    )(*operands)


def split_kernel(scal, line, payload):
    zh = scal[1]
    target = lax.broadcasted_iota(jnp.int32, (64, 128), 0)
    source = lax.broadcasted_iota(jnp.int32, (64, 128), 1)
    piece = target // 8 * 16 + (target & 7)
    ordered = (target & 31) // 4 * 16 + target // 32 * 4 + (target & 3)
    pick = [
        jnp.where(source == origin, F32(1), F32(0)).astype(BF)
        for origin in (piece, ordered, target + 8)
    ]
    both = jnp.concatenate(
        [
            dot(pick[0], line[1 - zh], NN),
            dot(pick[1], line[zh], NN),
            dot(pick[2], line[1 - zh], NN)[0:8],
        ],
        axis=0,
    ).astype(BF)
    for i in range(16):
        payload[i] = both


def split_call(*operands, interpret=False):
    return pl.pallas_call(
        split_kernel,
        out_shape=jax.ShapeDtypeStruct((16, 136, WIDTH), BF),
        in_specs=[SMEM, VMEM],
        out_specs=VMEM,
        compiler_params=room(16),
        interpret=interpret,
    )(*operands)


def layer_call(*operands, interpret=False):
    part = jax.ShapeDtypeStruct((16, 2, 24, 384), F32)
    sent = jax.ShapeDtypeStruct((16, 2, 24, 384), BF)
    return pl.pallas_call(
        layer_kernel,
        out_shape=(jax.ShapeDtypeStruct((TOK, WIDTH), F32), part, sent),
        in_specs=[SMEM] + [ANY] * 8 + [VMEM],
        out_specs=(VMEM,) * 3,
        scratch_shapes=[
            pltpu.VMEM((24, 32, TILE), BF),
            pltpu.VMEM((4, 6, 64, WIDTH), BF),
            pltpu.VMEM((4, 9, 64, WIDTH), BF),
            pltpu.VMEM((4, 3, 64, WIDTH), BF),
            pltpu.VMEM((WIDTH, WIDTH), BF),
            pltpu.VMEM((2 * WIDTH, WIDTH), BF),
            pltpu.VMEM((WIDTH, TOK), BF),
            pltpu.SemaphoreType.DMA((18,)),
        ],
        compiler_params=room(40),
        interpret=interpret,
    )(*operands)


def spread(block, axes, size):
    return lax.all_to_all(
        jnp.broadcast_to(block[None], (size,) + block.shape), axes, 0, 0, tiled=True
    )


def swap(value, axis):
    return lax.ppermute(value, axis, [(0, 1), (1, 0)])


def shards(tiles, counts, w_in, w_qkv, w_out, cotangent):
    rows = tiles[0]
    count = counts[0, 0]
    yx = lax.axis_index("y") * 4 + lax.axis_index("x")
    zl = lax.axis_index("zl")
    zh, core = lax.axis_index("zh"), lax.axis_index("core")
    w_out = w_out.T
    scal = jnp.stack([count, zh, core, yx * 64 + zl * 8]).astype(jnp.int32)
    own, ahead, even = prepare_call(scal, rows, w_in, w_qkv.T, w_out)
    line = lax.all_to_all(ahead.reshape(16, 16, WIDTH), Z, 0, 0, tiled=True)
    mate = swap(own, "core")
    partner = lax.ppermute(even, "zl", [(i, i ^ 1) for i in range(8)])
    line, mate, partner = lax.optimization_barrier((line.reshape(2, 128, WIDTH), mate, partner))
    got = lax.all_to_all(split_call(scal, line), YX, 0, 0, tiled=True)
    over_rest = got[:, 128:].reshape(128, WIDTH)
    cross, cross_rest = swap(got[:, :64], "core"), swap(over_rest, "core")
    out, keep, send = layer_call(
        scal,
        rows.reshape(4, 32, TILE),
        partner.reshape(2, 32, TILE),
        own.reshape(18, 64, WIDTH),
        mate.reshape(18, 64, WIDTH),
        got,
        cross,
        over_rest.reshape(2, 64, WIDTH),
        cross_rest.reshape(2, 64, WIDTH),
        cotangent[0],
    )
    pair = (keep + swap(send, "core").astype(F32)).astype(BF)
    plane = lax.all_to_all(pair, YX, 0, 0, tiled=True)
    plane = jnp.sum(plane.astype(F32), axis=0).astype(BF)
    column = jnp.broadcast_to(plane[:, None], (2, 8, 24, 384)).reshape(16, 24, 384)
    column = lax.all_to_all(column, Z, 0, 0, tiled=True)
    total = jnp.sum(column.astype(F32), axis=0)
    whole = spread(total.astype(BF), YX, 16).astype(F32)
    grad = whole.reshape(8, 2, 24, 384).transpose(0, 2, 1, 3).reshape(192, WIDTH)
    return (out[None], grad)


def solution(mesh):
    fine = Mesh(mesh.devices.reshape(4, 4, 8, 2, 2), ("y", "x", "zl", "zh", "core"))
    seq, slide = YX + ("zl",), ("zh", "core")
    placed = (
        P(slide, seq, None),
        P(slide, seq),
        P(slide, None),
        P(None, slide),
        P(None, slide),
        P(slide, seq, None),
    )
    return jax.shard_map(
        shards,
        mesh=fine,
        in_specs=placed,
        out_specs=(P(slide, seq, None), P(slide, None)),
        check_vma=False,
    )
```

```python
import jax
import jax.numpy as jnp
from jax import lax
from jax.experimental import pallas as pl
from jax.experimental.pallas import tpu as pltpu
from jax.sharding import Mesh
from jax.sharding import PartitionSpec as P

WIDTH = 768
TILE = 1536
HEADS = 16
HEAD = 48
DIL = 32
TOK = 128
FAR = 512
PACK = 1152
YX = ("y", "x")
Z = ("zh", "zl")
NT = (((1,), (1,)), ((), ()))
NN = (((1,), (0,)), ((), ()))
BF = jnp.bfloat16
F32 = jnp.float32
MARK = 64.0
LOW = -1e30
SCALE = HEAD**-0.5 / 0.6931471805599453


def dot(a, b, dims):
    return lax.dot_general(a, b, dims, preferred_element_type=F32)


def key_bias(block):
    lane = lax.broadcasted_iota(jnp.int32, (16, TOK), 1)
    pick = jnp.where(lane == 0, F32(1), F32(0)).astype(BF)
    return jnp.where(dot(pick, block[:, :TOK], NT)[0:1] > MARK / 2, F32(LOW), F32(0))


def layer_kernel(
    scal,
    rows,
    partner,
    own,
    mate,
    got,
    cross,
    over_rest,
    cross_rest,
    cot,
    out,
    keep,
    send,
    given,
    win,
    wqkv,
    wout,
    hid,
    kv,
    attn,
    sems,
):
    count, zh, core = scal[0], scal[1], scal[2]
    mine, other = zh * 2 + core, zh * 2 + 1 - core
    over, over_other = (1 - zh) * 2 + core, (1 - zh) * 2 + 1 - core
    arrived = got.at[:, pl.ds(0, 64)]
    moves = [
        (own.at[pl.ds(0, 6)], win.at[mine]),
        (mate.at[pl.ds(0, 6)], win.at[other]),
        (arrived.at[pl.ds(0, 6)], win.at[over]),
        (cross.at[pl.ds(0, 6)], win.at[over_other]),
        (rows, given.at[pl.ds(0, 4)]),
        (partner, given.at[pl.ds(4, 2)]),
        (got.at[:, pl.ds(64, 32)], given.at[pl.ds(8, 16), :, pl.ds(0, WIDTH)]),
        (got.at[:, pl.ds(96, 32)], given.at[pl.ds(8, 16), :, pl.ds(WIDTH, WIDTH)]),
        (own.at[pl.ds(6, 9)], wqkv.at[mine]),
        (mate.at[pl.ds(6, 9)], wqkv.at[other]),
        (arrived.at[pl.ds(6, 9)], wqkv.at[over]),
        (cross.at[pl.ds(6, 9)], wqkv.at[over_other]),
        (own.at[pl.ds(15, 3)], wout.at[mine]),
        (mate.at[pl.ds(15, 3)], wout.at[other]),
        (arrived.at[15], wout.at[over, 0]),
        (cross.at[15], wout.at[over_other, 0]),
        (over_rest, wout.at[over, pl.ds(1, 2)]),
        (cross_rest, wout.at[over_other, pl.ds(1, 2)]),
    ]
    copies = [pltpu.make_async_copy(s, d, sems.at[i]) for i, (s, d) in enumerate(moves)]
    for c in copies:
        c.start()
    given[pl.ds(6, 2)] = jnp.zeros((2, 32, TILE), BF)
    lane = lax.broadcasted_iota(jnp.int32, (1, TOK), 1)
    twice = jnp.where(lane & 1 == 0, F32(1), F32(0))
    for c in copies[:8]:
        c.wait()
    keys = given.reshape(WIDTH, TILE)
    hid[...] = dot(keys[...], win.reshape(TILE, WIDTH)[...], NN).astype(BF)
    bias = jnp.concatenate(
        [
            jnp.where(lane < count, twice, F32(LOW)),
            key_bias(keys[pl.ds(TOK, 64), :]),
            jnp.full((1, 64), LOW, F32),
            key_bias(keys[pl.ds(256, FAR), :]),
        ],
        axis=1,
    )
    for c in copies[8:12]:
        c.wait()
    flat = wqkv.reshape(3 * WIDTH, WIDTH)
    kv[...] = dot(flat[pl.ds(WIDTH, 2 * WIDTH), :], hid[...], NT).astype(BF)
    own_hid = hid[pl.ds(0, TOK), :]
    for h in range(HEADS):
        q = dot(own_hid, flat[pl.ds(h * HEAD, HEAD), :], NT).astype(BF)
        s = dot(q, kv[pl.ds(h * HEAD, HEAD), :], NN) * F32(SCALE) + bias
        p = jnp.exp2(s - jnp.max(s, axis=1, keepdims=True))
        o = dot(p.astype(BF), kv[pl.ds(WIDTH + h * HEAD, HEAD), :], NT)
        o = o / jnp.sum(p, axis=1, keepdims=True)
        attn[pl.ds(h * HEAD, HEAD), :] = o.T.astype(BF)
    cotangent = cot[...]
    token = lax.broadcasted_iota(jnp.int32, (192, TOK), 1)
    for which, target in ((core, keep), (1 - core, send)):
        for half in range(2):
            start = pl.multiple_of(half * 384 + which * 192, 192)
            block = attn[pl.ds(start, 192), :]
            block = jnp.where(token < count, block, jnp.zeros_like(block))
            part = dot(block, cotangent, NN)
            for r in range(8):
                for c in range(2):
                    target[r * 2 + c, half] = part[r * 24 : r * 24 + 24, c * 384 : c * 384 + 384].astype(
                        target.dtype
                    )
    for c in copies[12:]:
        c.wait()
    out[...] = dot(wout.reshape(WIDTH, WIDTH)[...], attn[...], NN).T


ANY = pl.BlockSpec(memory_space=pl.ANY)
VMEM = pl.BlockSpec(memory_space=pltpu.VMEM)
SMEM = pl.BlockSpec(memory_space=pltpu.SMEM)


def room(mebibytes):
    return pltpu.CompilerParams(vmem_limit_bytes=mebibytes * 1024 * 1024)


def prepare_kernel(scal, rows, w_in, w_qkv, w_out, own, ahead, even, sems):
    count, zh, at = scal[0], scal[1], scal[3]
    moves = [
        (w_in, own.at[pl.ds(0, 384)]),
        (w_qkv, own.at[pl.ds(384, 576)]),
        (w_out, own.at[pl.ds(960, 192)]),
    ]
    copies = [pltpu.make_async_copy(s, d, sems.at[i]) for i, (s, d) in enumerate(moves)]
    for c in copies:
        c.start()
    lane = lax.broadcasted_iota(jnp.int32, (1, TILE), 1)
    mark = jnp.where(lane == 0, F32(MARK), F32(0))
    distant = jnp.concatenate(
        [
            jnp.where(DIL * j < count, rows[pl.ds(DIL * j, 16), :].astype(F32)[0:1], mark)
            for j in range(4)
        ],
        axis=0,
    )
    row = lax.broadcasted_iota(jnp.int32, (TOK // 2, TOK), 0)
    source = lax.broadcasted_iota(jnp.int32, (TOK // 2, TOK), 1)
    pick = jnp.where((source == 2 * row) & (source < count), F32(1), F32(0)).astype(BF)
    marks = jnp.where(
        2 * lax.broadcasted_iota(jnp.int32, (TOK // 2, TILE), 0) < count, F32(0), mark
    )
    even[...] = (dot(pick, rows[...], NN) + marks).astype(BF)
    for c in copies:
        c.wait()
    start = pl.multiple_of(at // 16 * 16, 16)
    wide = own[pl.ds(start, 16), :].astype(F32)
    eight = jnp.where(at > start, wide[8:16], wide[0:8])
    far = jnp.concatenate([distant[:, :WIDTH], distant[:, WIDTH:]], axis=0)
    for half in range(2):
        value = jnp.where(zh == half, far, eight)
        ahead[half] = jnp.concatenate([value] * 8, axis=0).astype(BF)


def prepare_call(*operands, interpret=False):
    return pl.pallas_call(
        prepare_kernel,
        out_shape=(
            jax.ShapeDtypeStruct((PACK, WIDTH), BF),
            jax.ShapeDtypeStruct((2, 64, WIDTH), BF),
            jax.ShapeDtypeStruct((TOK // 2, TILE), BF),
        ),
        in_specs=[SMEM, VMEM] + [ANY] * 3,
        out_specs=(VMEM,) * 3,
        scratch_shapes=[pltpu.SemaphoreType.DMA((3,))],
        compiler_params=room(62),
        interpret=interpret,
    )(*operands)


def split_kernel(scal, line, payload):
    zh = scal[1]
    target = lax.broadcasted_iota(jnp.int32, (64, 64), 0)
    source = lax.broadcasted_iota(jnp.int32, (64, 64), 1)
    origin = (target & 31) // 4 * 8 + target // 32 * 4 + (target & 3)
    pick = jnp.where(source == origin, F32(1), F32(0)).astype(BF)
    both = jnp.concatenate([line[1 - zh], dot(pick, line[zh], NN).astype(BF)], axis=0)
    for i in range(16):
        payload[i] = both


def split_call(*operands, interpret=False):
    return pl.pallas_call(
        split_kernel,
        out_shape=jax.ShapeDtypeStruct((16, 128, WIDTH), BF),
        in_specs=[SMEM, VMEM],
        out_specs=VMEM,
        compiler_params=room(16),
        interpret=interpret,
    )(*operands)


def layer_call(*operands, interpret=False):
    part = jax.ShapeDtypeStruct((16, 2, 24, 384), F32)
    sent = jax.ShapeDtypeStruct((16, 2, 24, 384), BF)
    return pl.pallas_call(
        layer_kernel,
        out_shape=(jax.ShapeDtypeStruct((TOK, WIDTH), F32), part, sent),
        in_specs=[SMEM] + [ANY] * 8 + [VMEM],
        out_specs=(VMEM,) * 3,
        scratch_shapes=[
            pltpu.VMEM((24, 32, TILE), BF),
            pltpu.VMEM((4, 6, 64, WIDTH), BF),
            pltpu.VMEM((4, 9, 64, WIDTH), BF),
            pltpu.VMEM((4, 3, 64, WIDTH), BF),
            pltpu.VMEM((WIDTH, WIDTH), BF),
            pltpu.VMEM((2 * WIDTH, WIDTH), BF),
            pltpu.VMEM((WIDTH, TOK), BF),
            pltpu.SemaphoreType.DMA((18,)),
        ],
        compiler_params=room(40),
        interpret=interpret,
    )(*operands)


def spread(block, axes, size):
    return lax.all_to_all(
        jnp.broadcast_to(block[None], (size,) + block.shape), axes, 0, 0, tiled=True
    )


def swap(value, axis):
    return lax.ppermute(value, axis, [(0, 1), (1, 0)])


def shards(tiles, counts, w_in, w_qkv, w_out, cotangent):
    rows = tiles[0]
    count = counts[0, 0]
    yx = lax.axis_index("y") * 4 + lax.axis_index("x")
    zl = lax.axis_index("zl")
    zh, core = lax.axis_index("zh"), lax.axis_index("core")
    w_out = w_out.T
    scal = jnp.stack([count, zh, core, yx * 64 + zl * 8]).astype(jnp.int32)
    own, ahead, even = prepare_call(scal, rows, w_in, w_qkv.T, w_out)
    line = lax.all_to_all(ahead.reshape(16, 8, WIDTH), Z, 0, 0, tiled=True)
    mate = swap(own, "core")
    partner = lax.ppermute(even, "zl", [(i, i ^ 1) for i in range(8)])
    line, mate, partner = lax.optimization_barrier((line.reshape(2, 64, WIDTH), mate, partner))
    got = lax.all_to_all(split_call(scal, line), YX, 0, 0, tiled=True)
    over_rest = swap(w_out[64:], "zh")
    cross_rest = swap(over_rest, "core")
    got, over_rest, cross_rest = lax.optimization_barrier((got, over_rest, cross_rest))
    cross = swap(got[:, :64], "core")
    out, keep, send = layer_call(
        scal,
        rows.reshape(4, 32, TILE),
        partner.reshape(2, 32, TILE),
        own.reshape(18, 64, WIDTH),
        mate.reshape(18, 64, WIDTH),
        got,
        cross,
        over_rest.reshape(2, 64, WIDTH),
        cross_rest.reshape(2, 64, WIDTH),
        cotangent[0],
    )
    pair = (keep + swap(send, "core").astype(F32)).astype(BF)
    plane = lax.all_to_all(pair, YX, 0, 0, tiled=True)
    plane = jnp.sum(plane.astype(F32), axis=0).astype(BF)
    column = jnp.broadcast_to(plane[:, None], (2, 8, 24, 384)).reshape(16, 24, 384)
    column = lax.all_to_all(column, Z, 0, 0, tiled=True)
    total = jnp.sum(column.astype(F32), axis=0)
    whole = spread(total.astype(BF), YX, 16).astype(F32)
    grad = whole.reshape(8, 2, 24, 384).transpose(0, 2, 1, 3).reshape(192, WIDTH)
    return (out[None], grad)


def solution(mesh):
    fine = Mesh(mesh.devices.reshape(4, 4, 8, 2, 2), ("y", "x", "zl", "zh", "core"))
    seq, slide = YX + ("zl",), ("zh", "core")
    placed = (
        P(slide, seq, None),
        P(slide, seq),
        P(slide, None),
        P(None, slide),
        P(None, slide),
        P(slide, seq, None),
    )
    return jax.shard_map(
        shards,
        mesh=fine,
        in_specs=placed,
        out_specs=(P(slide, seq, None), P(slide, None)),
        check_vma=False,
    )
```

```python
import jax
import jax.numpy as jnp
from jax import lax
from jax.experimental import pallas as pl
from jax.experimental.pallas import tpu as pltpu
from jax.sharding import Mesh
from jax.sharding import PartitionSpec as P

WIDTH = 768
TILE = 1536
HEADS = 16
HEAD = 48
DIL = 32
TOK = 128
FAR = 512
PACK = 1152
YX = ("y", "x")
Z = ("zh", "zl")
NT = (((1,), (1,)), ((), ()))
NN = (((1,), (0,)), ((), ()))
BF = jnp.bfloat16
F32 = jnp.float32
MARK = 64.0
LOW = -1e30
SCALE = HEAD**-0.5 / 0.6931471805599453


def dot(a, b, dims):
    return lax.dot_general(a, b, dims, preferred_element_type=F32)


def key_bias(block):
    lane = lax.broadcasted_iota(jnp.int32, (16, TOK), 1)
    pick = jnp.where(lane == 0, F32(1), F32(0)).astype(BF)
    return jnp.where(dot(pick, block[:, :TOK], NT)[0:1] > MARK / 2, F32(LOW), F32(0))


def layer_kernel(
    scal,
    rows,
    partner,
    own,
    mate,
    got,
    cross,
    over_rest,
    cross_rest,
    cot,
    out,
    keep,
    send,
    given,
    win,
    wqkv,
    wout,
    hid,
    kv,
    attn,
    sems,
):
    count, zh, core = scal[0], scal[1], scal[2]
    mine, other = zh * 2 + core, zh * 2 + 1 - core
    over, over_other = (1 - zh) * 2 + core, (1 - zh) * 2 + 1 - core
    arrived = got.at[:, pl.ds(0, 64)]
    moves = [
        (own.at[pl.ds(0, 6)], win.at[mine]),
        (mate.at[pl.ds(0, 6)], win.at[other]),
        (arrived.at[pl.ds(0, 6)], win.at[over]),
        (cross.at[pl.ds(0, 6)], win.at[over_other]),
        (rows, given.at[pl.ds(0, 4)]),
        (partner, given.at[pl.ds(4, 2)]),
        (got.at[:, pl.ds(64, 32)], given.at[pl.ds(8, 16), :, pl.ds(0, WIDTH)]),
        (got.at[:, pl.ds(96, 32)], given.at[pl.ds(8, 16), :, pl.ds(WIDTH, WIDTH)]),
        (own.at[pl.ds(6, 9)], wqkv.at[mine]),
        (mate.at[pl.ds(6, 9)], wqkv.at[other]),
        (arrived.at[pl.ds(6, 9)], wqkv.at[over]),
        (cross.at[pl.ds(6, 9)], wqkv.at[over_other]),
        (own.at[pl.ds(15, 3)], wout.at[mine]),
        (mate.at[pl.ds(15, 3)], wout.at[other]),
        (arrived.at[15], wout.at[over, 0]),
        (cross.at[15], wout.at[over_other, 0]),
        (over_rest, wout.at[over, pl.ds(1, 2)]),
        (cross_rest, wout.at[over_other, pl.ds(1, 2)]),
    ]
    copies = [pltpu.make_async_copy(s, d, sems.at[i]) for i, (s, d) in enumerate(moves)]
    for c in copies:
        c.start()
    given[pl.ds(6, 2)] = jnp.zeros((2, 32, TILE), BF)
    lane = lax.broadcasted_iota(jnp.int32, (1, TOK), 1)
    twice = jnp.where(lane & 1 == 0, F32(1), F32(0))
    for c in copies[:8]:
        c.wait()
    keys = given.reshape(WIDTH, TILE)
    hid[...] = dot(keys[...], win.reshape(TILE, WIDTH)[...], NN).astype(BF)
    bias = jnp.concatenate(
        [
            jnp.where(lane < count, twice, F32(LOW)),
            key_bias(keys[pl.ds(TOK, 64), :]),
            jnp.full((1, 64), LOW, F32),
            key_bias(keys[pl.ds(256, FAR), :]),
        ],
        axis=1,
    )
    for c in copies[8:12]:
        c.wait()
    flat = wqkv.reshape(3 * WIDTH, WIDTH)
    kv[...] = dot(flat[pl.ds(WIDTH, 2 * WIDTH), :], hid[...], NT).astype(BF)
    own_hid = hid[pl.ds(0, TOK), :]
    for h in range(HEADS):
        q = dot(own_hid, flat[pl.ds(h * HEAD, HEAD), :], NT).astype(BF)
        s = dot(q, kv[pl.ds(h * HEAD, HEAD), :], NN) * F32(SCALE) + bias
        p = jnp.exp2(s - jnp.max(s, axis=1, keepdims=True))
        o = dot(p.astype(BF), kv[pl.ds(WIDTH + h * HEAD, HEAD), :], NT)
        o = o / jnp.sum(p, axis=1, keepdims=True)
        attn[pl.ds(h * HEAD, HEAD), :] = o.T.astype(BF)
    cotangent = cot[...]
    token = lax.broadcasted_iota(jnp.int32, (192, TOK), 1)
    for which, target in ((core, keep), (1 - core, send)):
        for half in range(2):
            start = pl.multiple_of(half * 384 + which * 192, 192)
            block = attn[pl.ds(start, 192), :]
            block = jnp.where(token < count, block, jnp.zeros_like(block))
            part = dot(block, cotangent, NN)
            for r in range(8):
                for c in range(2):
                    target[r * 2 + c, half] = part[r * 24 : r * 24 + 24, c * 384 : c * 384 + 384].astype(
                        target.dtype
                    )
    for c in copies[12:]:
        c.wait()
    out[...] = dot(wout.reshape(WIDTH, WIDTH)[...], attn[...], NN).T


ANY = pl.BlockSpec(memory_space=pl.ANY)
VMEM = pl.BlockSpec(memory_space=pltpu.VMEM)
SMEM = pl.BlockSpec(memory_space=pltpu.SMEM)


def room(mebibytes):
    return pltpu.CompilerParams(vmem_limit_bytes=mebibytes * 1024 * 1024)


def prepare_kernel(scal, rows, w_in, w_qkv, w_out, own, ahead, even, sems):
    count, zh, at = scal[0], scal[1], scal[3]
    moves = [
        (w_in, own.at[pl.ds(0, 384)]),
        (w_qkv, own.at[pl.ds(384, 576)]),
        (w_out, own.at[pl.ds(960, 192)]),
    ]
    copies = [pltpu.make_async_copy(s, d, sems.at[i]) for i, (s, d) in enumerate(moves)]
    for c in copies:
        c.start()
    lane = lax.broadcasted_iota(jnp.int32, (1, TILE), 1)
    mark = jnp.where(lane == 0, F32(MARK), F32(0))
    distant = jnp.concatenate(
        [
            jnp.where(DIL * j < count, rows[pl.ds(DIL * j, 16), :].astype(F32)[0:1], mark)
            for j in range(4)
        ],
        axis=0,
    )
    row = lax.broadcasted_iota(jnp.int32, (TOK // 2, TOK), 0)
    source = lax.broadcasted_iota(jnp.int32, (TOK // 2, TOK), 1)
    pick = jnp.where((source == 2 * row) & (source < count), F32(1), F32(0)).astype(BF)
    marks = jnp.where(
        2 * lax.broadcasted_iota(jnp.int32, (TOK // 2, TILE), 0) < count, F32(0), mark
    )
    even[...] = (dot(pick, rows[...], NN) + marks).astype(BF)
    for c in copies:
        c.wait()
    start = pl.multiple_of(at // 16 * 16, 16)
    wide = own[pl.ds(start, 16), :].astype(F32)
    eight = jnp.where(at > start, wide[8:16], wide[0:8])
    line = 1024 + at // 64 * 8 + at // 8 % 8
    start = pl.multiple_of(line // 16 * 16, 16)
    wide = own[pl.ds(start, 16), :].astype(F32)
    single = lax.broadcasted_iota(jnp.int32, (16, WIDTH), 0) == line - start
    ninth = jnp.sum(jnp.where(single, wide, F32(0)), axis=0, keepdims=True)
    far = jnp.concatenate([distant[:, :WIDTH], distant[:, WIDTH:]], axis=0)
    spare = jnp.zeros((2, TOK), F32)
    for half in range(2):
        value = jnp.where(zh == half, far, eight)
        lanes = [value[:, c * TOK : (c + 1) * TOK] for c in range(6)]
        more = [ninth[:, c * TOK : (c + 1) * TOK] for c in range(6)]
        block = jnp.concatenate(lanes + [jnp.concatenate(more + [spare], axis=0)], axis=0)
        ahead[half] = jnp.concatenate([block] * 8, axis=0).astype(BF)


def prepare_call(*operands, interpret=False):
    return pl.pallas_call(
        prepare_kernel,
        out_shape=(
            jax.ShapeDtypeStruct((PACK, WIDTH), BF),
            jax.ShapeDtypeStruct((2, 448, TOK), BF),
            jax.ShapeDtypeStruct((TOK // 2, TILE), BF),
        ),
        in_specs=[SMEM, VMEM] + [ANY] * 3,
        out_specs=(VMEM,) * 3,
        scratch_shapes=[pltpu.SemaphoreType.DMA((3,))],
        compiler_params=room(62),
        interpret=interpret,
    )(*operands)


def split_kernel(scal, line, payload):
    zh = scal[1]
    ours, theirs = line[zh], line[1 - zh]
    target = lax.broadcasted_iota(jnp.int32, (64, 448), 0)
    source = lax.broadcasted_iota(jnp.int32, (64, 448), 1)
    piece = target // 8 * 56 + (target & 7)
    ordered = (target & 31) // 4 * 56 + target // 32 * 4 + (target & 3)
    rest = (target & 7) * 56 + 48
    columns = []
    for c in range(6):
        picks = [
            jnp.where(source == origin, F32(1), F32(0)).astype(BF)
            for origin in (piece + 8 * c, ordered + 8 * c, rest + c)
        ]
        columns.append(
            jnp.concatenate(
                [
                    dot(picks[0], theirs, NN),
                    dot(picks[1], ours, NN),
                    dot(picks[2], theirs, NN)[0:8],
                ],
                axis=0,
            )
        )
    both = jnp.concatenate(columns, axis=1).astype(BF)
    for i in range(16):
        payload[i] = both


def split_call(*operands, interpret=False):
    return pl.pallas_call(
        split_kernel,
        out_shape=jax.ShapeDtypeStruct((16, 136, WIDTH), BF),
        in_specs=[SMEM, VMEM],
        out_specs=VMEM,
        compiler_params=room(16),
        interpret=interpret,
    )(*operands)


def layer_call(*operands, interpret=False):
    part = jax.ShapeDtypeStruct((16, 2, 24, 384), F32)
    sent = jax.ShapeDtypeStruct((16, 2, 24, 384), BF)
    return pl.pallas_call(
        layer_kernel,
        out_shape=(jax.ShapeDtypeStruct((TOK, WIDTH), F32), part, sent),
        in_specs=[SMEM] + [ANY] * 8 + [VMEM],
        out_specs=(VMEM,) * 3,
        scratch_shapes=[
            pltpu.VMEM((24, 32, TILE), BF),
            pltpu.VMEM((4, 6, 64, WIDTH), BF),
            pltpu.VMEM((4, 9, 64, WIDTH), BF),
            pltpu.VMEM((4, 3, 64, WIDTH), BF),
            pltpu.VMEM((WIDTH, WIDTH), BF),
            pltpu.VMEM((2 * WIDTH, WIDTH), BF),
            pltpu.VMEM((WIDTH, TOK), BF),
            pltpu.SemaphoreType.DMA((18,)),
        ],
        compiler_params=room(40),
        interpret=interpret,
    )(*operands)


def spread(block, axes, size):
    return lax.all_to_all(
        jnp.broadcast_to(block[None], (size,) + block.shape), axes, 0, 0, tiled=True
    )


def swap(value, axis):
    return lax.ppermute(value, axis, [(0, 1), (1, 0)])


def shards(tiles, counts, w_in, w_qkv, w_out, cotangent):
    rows = tiles[0]
    count = counts[0, 0]
    yx = lax.axis_index("y") * 4 + lax.axis_index("x")
    zl = lax.axis_index("zl")
    zh, core = lax.axis_index("zh"), lax.axis_index("core")
    w_out = w_out.T
    scal = jnp.stack([count, zh, core, yx * 64 + zl * 8]).astype(jnp.int32)
    own, ahead, even = prepare_call(scal, rows, w_in, w_qkv.T, w_out)
    line = lax.all_to_all(ahead.reshape(16, 56, TOK), Z, 0, 0, tiled=True)
    mate = swap(own, "core")
    partner = lax.ppermute(even, "zl", [(i, i ^ 1) for i in range(8)])
    line, mate, partner = lax.optimization_barrier((line.reshape(2, 448, TOK), mate, partner))
    got = lax.all_to_all(split_call(scal, line), YX, 0, 0, tiled=True)
    over_rest = got[:, 128:].reshape(128, WIDTH)
    cross, cross_rest = swap(got[:, :64], "core"), swap(over_rest, "core")
    out, keep, send = layer_call(
        scal,
        rows.reshape(4, 32, TILE),
        partner.reshape(2, 32, TILE),
        own.reshape(18, 64, WIDTH),
        mate.reshape(18, 64, WIDTH),
        got,
        cross,
        over_rest.reshape(2, 64, WIDTH),
        cross_rest.reshape(2, 64, WIDTH),
        cotangent[0],
    )
    pair = (keep + swap(send, "core").astype(F32)).astype(BF)
    plane = lax.all_to_all(pair, YX, 0, 0, tiled=True)
    plane = jnp.sum(plane.astype(F32), axis=0).astype(BF)
    column = jnp.broadcast_to(plane[:, None], (2, 8, 24, 384)).reshape(16, 24, 384)
    column = lax.all_to_all(column, Z, 0, 0, tiled=True)
    total = jnp.sum(column.astype(F32), axis=0)
    whole = spread(total.astype(BF), YX, 16).astype(F32)
    grad = whole.reshape(8, 2, 24, 384).transpose(0, 2, 1, 3).reshape(192, WIDTH)
    return (out[None], grad)


def solution(mesh):
    fine = Mesh(mesh.devices.reshape(4, 4, 8, 2, 2), ("y", "x", "zl", "zh", "core"))
    seq, slide = YX + ("zl",), ("zh", "core")
    placed = (
        P(slide, seq, None),
        P(slide, seq),
        P(slide, None),
        P(None, slide),
        P(None, slide),
        P(slide, seq, None),
    )
    return jax.shard_map(
        shards,
        mesh=fine,
        in_specs=placed,
        out_specs=(P(slide, seq, None), P(slide, None)),
        check_vma=False,
    )
```

```python
import jax
import jax.numpy as jnp
from jax import lax
from jax.experimental import pallas as pl
from jax.experimental.pallas import tpu as pltpu
from jax.sharding import Mesh
from jax.sharding import PartitionSpec as P

WIDTH = 768
TILE = 1536
HEADS = 16
HEAD = 48
DIL = 32
TOK = 128
FAR = 512
PACK = 1152
YX = ("y", "x")
Z = ("zh", "zl")
NT = (((1,), (1,)), ((), ()))
NN = (((1,), (0,)), ((), ()))
BF = jnp.bfloat16
F32 = jnp.float32
MARK = 64.0
LOW = -1e30
SCALE = HEAD**-0.5 / 0.6931471805599453


def dot(a, b, dims):
    return lax.dot_general(a, b, dims, preferred_element_type=F32)


def key_bias(block):
    lane = lax.broadcasted_iota(jnp.int32, (16, TOK), 1)
    pick = jnp.where(lane == 0, F32(1), F32(0)).astype(BF)
    return jnp.where(dot(pick, block[:, :TOK], NT)[0:1] > MARK / 2, F32(LOW), F32(0))


def begin_kernel(scal, rows, partner, own, mate, got, partial, last, bias, given, win, sems):
    count, zh, core = scal[0], scal[1], scal[2]
    moves = [
        (own.at[pl.ds(0, 6)], win.at[0]),
        (mate.at[pl.ds(0, 6)], win.at[1]),
        (got.at[pl.ds(0, 6), pl.ds(0, 64)], win.at[2]),
        (rows, given.at[pl.ds(0, 4)]),
        (partner, given.at[pl.ds(4, 2)]),
        (got.at[:, pl.ds(64, 32)], given.at[pl.ds(8, 16), :, pl.ds(0, WIDTH)]),
        (got.at[:, pl.ds(96, 32)], given.at[pl.ds(8, 16), :, pl.ds(WIDTH, WIDTH)]),
    ]
    copies = [pltpu.make_async_copy(s, d, sems.at[i]) for i, (s, d) in enumerate(moves)]
    for c in copies:
        c.start()
    given[pl.ds(6, 2)] = jnp.zeros((2, 32, TILE), BF)
    for c in copies:
        c.wait()

    def columns(shard):
        start = pl.multiple_of(shard * 384, 384)
        return given[:, :, pl.ds(start, 384)].reshape(WIDTH, 384)

    shards_here = (zh * 2 + core, zh * 2 + 1 - core, (1 - zh) * 2 + core)
    parts = [
        dot(columns(s), win[i].reshape(384, WIDTH), NN) for i, s in enumerate(shards_here)
    ]
    partial[...] = parts[0] + parts[1] + parts[2]
    last[...] = columns((1 - zh) * 2 + 1 - core)
    lane = lax.broadcasted_iota(jnp.int32, (1, TOK), 1)
    twice = jnp.where(lane & 1 == 0, F32(1), F32(0))
    keys = given.reshape(WIDTH, TILE)
    bias[...] = jnp.concatenate(
        [
            jnp.where(lane < count, twice, F32(LOW)),
            key_bias(keys[pl.ds(TOK, 64), :]),
            jnp.full((1, 64), LOW, F32),
            key_bias(keys[pl.ds(256, FAR), :]),
        ],
        axis=1,
    )


def layer_kernel(
    scal,
    partial,
    last,
    key_bias_row,
    own,
    mate,
    got,
    cross,
    over_rest,
    cross_rest,
    cot,
    out,
    keep,
    send,
    win,
    wqkv,
    wout,
    hid,
    kv,
    attn,
    sems,
):
    count, zh, core = scal[0], scal[1], scal[2]
    mine, other = zh * 2 + core, zh * 2 + 1 - core
    over, over_other = (1 - zh) * 2 + core, (1 - zh) * 2 + 1 - core
    arrived = got.at[:, pl.ds(0, 64)]
    moves = [
        (cross.at[pl.ds(0, 6)], win),
        (own.at[pl.ds(6, 9)], wqkv.at[mine]),
        (mate.at[pl.ds(6, 9)], wqkv.at[other]),
        (arrived.at[pl.ds(6, 9)], wqkv.at[over]),
        (cross.at[pl.ds(6, 9)], wqkv.at[over_other]),
        (own.at[pl.ds(15, 3)], wout.at[mine]),
        (mate.at[pl.ds(15, 3)], wout.at[other]),
        (arrived.at[15], wout.at[over, 0]),
        (cross.at[15], wout.at[over_other, 0]),
        (over_rest, wout.at[over, pl.ds(1, 2)]),
        (cross_rest, wout.at[over_other, pl.ds(1, 2)]),
    ]
    copies = [pltpu.make_async_copy(s, d, sems.at[i]) for i, (s, d) in enumerate(moves)]
    for c in copies:
        c.start()
    copies[0].wait()
    fourth = dot(last[...], win[...].reshape(384, WIDTH), NN)
    hid[...] = (partial[...] + fourth).astype(BF)
    bias = key_bias_row[...]
    for c in copies[1:5]:
        c.wait()
    flat = wqkv.reshape(3 * WIDTH, WIDTH)
    kv[...] = dot(flat[pl.ds(WIDTH, 2 * WIDTH), :], hid[...], NT).astype(BF)
    own_hid = hid[pl.ds(0, TOK), :]
    for h in range(HEADS):
        q = dot(own_hid, flat[pl.ds(h * HEAD, HEAD), :], NT).astype(BF)
        s = dot(q, kv[pl.ds(h * HEAD, HEAD), :], NN) * F32(SCALE) + bias
        p = jnp.exp2(s - jnp.max(s, axis=1, keepdims=True))
        o = dot(p.astype(BF), kv[pl.ds(WIDTH + h * HEAD, HEAD), :], NT)
        o = o / jnp.sum(p, axis=1, keepdims=True)
        attn[pl.ds(h * HEAD, HEAD), :] = o.T.astype(BF)
    cotangent = cot[...]
    token = lax.broadcasted_iota(jnp.int32, (192, TOK), 1)
    for which, target in ((core, keep), (1 - core, send)):
        for half in range(2):
            start = pl.multiple_of(half * 384 + which * 192, 192)
            block = attn[pl.ds(start, 192), :]
            block = jnp.where(token < count, block, jnp.zeros_like(block))
            part = dot(block, cotangent, NN)
            for r in range(8):
                for c in range(2):
                    target[r * 2 + c, half] = part[r * 24 : r * 24 + 24, c * 384 : c * 384 + 384].astype(
                        target.dtype
                    )
    for c in copies[5:]:
        c.wait()
    out[...] = dot(wout.reshape(WIDTH, WIDTH)[...], attn[...], NN).T


ANY = pl.BlockSpec(memory_space=pl.ANY)
VMEM = pl.BlockSpec(memory_space=pltpu.VMEM)
SMEM = pl.BlockSpec(memory_space=pltpu.SMEM)


def room(mebibytes):
    return pltpu.CompilerParams(vmem_limit_bytes=mebibytes * 1024 * 1024)


def prepare_kernel(scal, rows, w_in, w_qkv, w_out, pack, ahead, even, own, sems):
    count, zh, at = scal[0], scal[1], scal[3]
    moves = [
        (w_in, own.at[pl.ds(0, 384)]),
        (w_qkv, own.at[pl.ds(384, 576)]),
        (w_out, own.at[pl.ds(960, 192)]),
    ]
    copies = [pltpu.make_async_copy(s, d, sems.at[i]) for i, (s, d) in enumerate(moves)]
    for c in copies:
        c.start()
    lane = lax.broadcasted_iota(jnp.int32, (1, TILE), 1)
    mark = jnp.where(lane == 0, F32(MARK), F32(0))
    distant = jnp.concatenate(
        [
            jnp.where(DIL * j < count, rows[pl.ds(DIL * j, 16), :].astype(F32)[0:1], mark)
            for j in range(4)
        ],
        axis=0,
    )
    row = lax.broadcasted_iota(jnp.int32, (TOK // 2, TOK), 0)
    source = lax.broadcasted_iota(jnp.int32, (TOK // 2, TOK), 1)
    pick = jnp.where((source == 2 * row) & (source < count), F32(1), F32(0)).astype(BF)
    marks = jnp.where(
        2 * lax.broadcasted_iota(jnp.int32, (TOK // 2, TILE), 0) < count, F32(0), mark
    )
    even[...] = (dot(pick, rows[...], NN) + marks).astype(BF)
    for c in copies:
        c.wait()
    back = pltpu.make_async_copy(own, pack, sems.at[3])
    back.start()
    start = pl.multiple_of(at // 16 * 16, 16)
    wide = own[pl.ds(start, 16), :].astype(F32)
    eight = jnp.where(at > start, wide[8:16], wide[0:8])
    line = 1024 + at // 64 * 8 + at // 8 % 8
    start = pl.multiple_of(line // 16 * 16, 16)
    wide = own[pl.ds(start, 16), :].astype(F32)
    single = lax.broadcasted_iota(jnp.int32, (16, WIDTH), 0) == line - start
    ninth = jnp.sum(jnp.where(single, wide, F32(0)), axis=0, keepdims=True)
    far = jnp.concatenate([distant[:, :WIDTH], distant[:, WIDTH:]], axis=0)
    spare = jnp.zeros((2, TOK), F32)
    for half in range(2):
        value = jnp.where(zh == half, far, eight)
        lanes = [value[:, c * TOK : (c + 1) * TOK] for c in range(6)]
        more = [ninth[:, c * TOK : (c + 1) * TOK] for c in range(6)]
        block = jnp.concatenate(lanes + [jnp.concatenate(more + [spare], axis=0)], axis=0)
        ahead[half] = jnp.concatenate([block] * 8, axis=0).astype(BF)
    back.wait()


def prepare_call(*operands, interpret=False):
    return pl.pallas_call(
        prepare_kernel,
        out_shape=(
            jax.ShapeDtypeStruct((PACK, WIDTH), BF),
            jax.ShapeDtypeStruct((2, 448, TOK), BF),
            jax.ShapeDtypeStruct((TOK // 2, TILE), BF),
        ),
        in_specs=[SMEM, VMEM] + [ANY] * 3,
        out_specs=(ANY, VMEM, VMEM),
        scratch_shapes=[pltpu.VMEM((PACK, WIDTH), BF), pltpu.SemaphoreType.DMA((4,))],
        compiler_params=room(62),
        interpret=interpret,
    )(*operands)


def split_kernel(scal, line, payload):
    zh = scal[1]
    ours, theirs = line[zh], line[1 - zh]
    target = lax.broadcasted_iota(jnp.int32, (64, 448), 0)
    source = lax.broadcasted_iota(jnp.int32, (64, 448), 1)
    piece = target // 8 * 56 + (target & 7)
    ordered = (target & 31) // 4 * 56 + target // 32 * 4 + (target & 3)
    rest = (target & 7) * 56 + 48
    columns = []
    for c in range(6):
        picks = [
            jnp.where(source == origin, F32(1), F32(0)).astype(BF)
            for origin in (piece + 8 * c, ordered + 8 * c, rest + c)
        ]
        columns.append(
            jnp.concatenate(
                [
                    dot(picks[0], theirs, NN),
                    dot(picks[1], ours, NN),
                    dot(picks[2], theirs, NN)[0:8],
                ],
                axis=0,
            )
        )
    both = jnp.concatenate(columns, axis=1).astype(BF)
    for i in range(16):
        payload[i] = both


def split_call(*operands, interpret=False):
    return pl.pallas_call(
        split_kernel,
        out_shape=jax.ShapeDtypeStruct((16, 136, WIDTH), BF),
        in_specs=[SMEM, VMEM],
        out_specs=VMEM,
        compiler_params=room(16),
        interpret=interpret,
    )(*operands)


def begin_call(*operands, interpret=False):
    return pl.pallas_call(
        begin_kernel,
        out_shape=(
            jax.ShapeDtypeStruct((WIDTH, WIDTH), F32),
            jax.ShapeDtypeStruct((WIDTH, 384), BF),
            jax.ShapeDtypeStruct((1, WIDTH), F32),
        ),
        in_specs=[SMEM] + [ANY] * 5,
        out_specs=(VMEM,) * 3,
        scratch_shapes=[
            pltpu.VMEM((24, 32, TILE), BF),
            pltpu.VMEM((3, 6, 64, WIDTH), BF),
            pltpu.SemaphoreType.DMA((7,)),
        ],
        compiler_params=room(32),
        interpret=interpret,
    )(*operands)


def layer_call(*operands, interpret=False):
    part = jax.ShapeDtypeStruct((16, 2, 24, 384), F32)
    sent = jax.ShapeDtypeStruct((16, 2, 24, 384), BF)
    return pl.pallas_call(
        layer_kernel,
        out_shape=(jax.ShapeDtypeStruct((TOK, WIDTH), F32), part, sent),
        in_specs=[SMEM] + [VMEM] * 3 + [ANY] * 6 + [VMEM],
        out_specs=(VMEM,) * 3,
        scratch_shapes=[
            pltpu.VMEM((6, 64, WIDTH), BF),
            pltpu.VMEM((4, 9, 64, WIDTH), BF),
            pltpu.VMEM((4, 3, 64, WIDTH), BF),
            pltpu.VMEM((WIDTH, WIDTH), BF),
            pltpu.VMEM((2 * WIDTH, WIDTH), BF),
            pltpu.VMEM((WIDTH, TOK), BF),
            pltpu.SemaphoreType.DMA((11,)),
        ],
        compiler_params=room(40),
        interpret=interpret,
    )(*operands)


def spread(block, axes, size):
    return lax.all_to_all(
        jnp.broadcast_to(block[None], (size,) + block.shape), axes, 0, 0, tiled=True
    )


def swap(value, axis):
    return lax.ppermute(value, axis, [(0, 1), (1, 0)])


def shards(tiles, counts, w_in, w_qkv, w_out, cotangent):
    rows = tiles[0]
    count = counts[0, 0]
    yx = lax.axis_index("y") * 4 + lax.axis_index("x")
    zl = lax.axis_index("zl")
    zh, core = lax.axis_index("zh"), lax.axis_index("core")
    w_out = w_out.T
    scal = jnp.stack([count, zh, core, yx * 64 + zl * 8]).astype(jnp.int32)
    own, ahead, even = prepare_call(scal, rows, w_in, w_qkv.T, w_out)
    line = lax.all_to_all(ahead.reshape(16, 56, TOK), Z, 0, 0, tiled=True)
    mate = swap(own, "core")
    partner = lax.ppermute(even, "zl", [(i, i ^ 1) for i in range(8)])
    line, mate, partner = lax.optimization_barrier((line.reshape(2, 448, TOK), mate, partner))
    got = lax.all_to_all(split_call(scal, line), YX, 0, 0, tiled=True)
    over_rest = got[:, 128:].reshape(128, WIDTH)
    cross, cross_rest = swap(got[:, :64], "core"), swap(over_rest, "core")
    own, mate = own.reshape(18, 64, WIDTH), mate.reshape(18, 64, WIDTH)
    state = begin_call(
        scal, rows.reshape(4, 32, TILE), partner.reshape(2, 32, TILE), own, mate, got
    )
    over_rest, cross_rest = over_rest.reshape(2, 64, WIDTH), cross_rest.reshape(2, 64, WIDTH)
    out, keep, send = layer_call(
        scal, *state, own, mate, got, cross, over_rest, cross_rest, cotangent[0]
    )
    pair = (keep + swap(send, "core").astype(F32)).astype(BF)
    plane = lax.all_to_all(pair, YX, 0, 0, tiled=True)
    plane = jnp.sum(plane.astype(F32), axis=0).astype(BF)
    column = jnp.broadcast_to(plane[:, None], (2, 8, 24, 384)).reshape(16, 24, 384)
    column = lax.all_to_all(column, Z, 0, 0, tiled=True)
    total = jnp.sum(column.astype(F32), axis=0)
    whole = spread(total.astype(BF), YX, 16).astype(F32)
    grad = whole.reshape(8, 2, 24, 384).transpose(0, 2, 1, 3).reshape(192, WIDTH)
    return (out[None], grad)


def solution(mesh):
    fine = Mesh(mesh.devices.reshape(4, 4, 8, 2, 2), ("y", "x", "zl", "zh", "core"))
    seq, slide = YX + ("zl",), ("zh", "core")
    placed = (
        P(slide, seq, None),
        P(slide, seq),
        P(slide, None),
        P(None, slide),
        P(None, slide),
        P(slide, seq, None),
    )
    return jax.shard_map(
        shards,
        mesh=fine,
        in_specs=placed,
        out_specs=(P(slide, seq, None), P(slide, None)),
        check_vma=False,
    )
```

```python
import jax
import jax.numpy as jnp
from jax import lax
from jax.experimental import pallas as pl
from jax.experimental.pallas import tpu as pltpu
from jax.sharding import Mesh
from jax.sharding import PartitionSpec as P

WIDTH = 768
TILE = 1536
HEADS = 16
HEAD = 48
DIL = 32
TOK = 128
FAR = 512
PACK = 1152
YX = ("y", "x")
Z = ("zh", "zl")
NT = (((1,), (1,)), ((), ()))
NN = (((1,), (0,)), ((), ()))
BF = jnp.bfloat16
F32 = jnp.float32
MARK = 64.0
LOW = -1e30
SCALE = HEAD**-0.5 / 0.6931471805599453


def dot(a, b, dims):
    return lax.dot_general(a, b, dims, preferred_element_type=F32)


def key_bias(block):
    lane = lax.broadcasted_iota(jnp.int32, (16, TOK), 1)
    pick = jnp.where(lane == 0, F32(1), F32(0)).astype(BF)
    return jnp.where(dot(pick, block[:, :TOK], NT)[0:1] > MARK / 2, F32(LOW), F32(0))


def begin_kernel(scal, rows, partner, own, mate, over, far, partial, last, bias, given, win, sems):
    count, zh, core = scal[0], scal[1], scal[2]
    moves = [
        (own.at[pl.ds(0, 6)], win.at[0]),
        (mate.at[pl.ds(0, 6)], win.at[1]),
        (over.at[pl.ds(0, 6)], win.at[2]),
        (rows, given.at[pl.ds(0, 4)]),
        (partner, given.at[pl.ds(4, 2)]),
        (far.at[:, pl.ds(0, 32)], given.at[pl.ds(8, 16), :, pl.ds(0, WIDTH)]),
        (far.at[:, pl.ds(32, 32)], given.at[pl.ds(8, 16), :, pl.ds(WIDTH, WIDTH)]),
    ]
    copies = [pltpu.make_async_copy(s, d, sems.at[i]) for i, (s, d) in enumerate(moves)]
    for c in copies:
        c.start()
    given[pl.ds(6, 2)] = jnp.zeros((2, 32, TILE), BF)
    for c in copies:
        c.wait()

    def columns(shard):
        start = pl.multiple_of(shard * 384, 384)
        return given[:, :, pl.ds(start, 384)].reshape(WIDTH, 384)

    shards_here = (zh * 2 + core, zh * 2 + 1 - core, (1 - zh) * 2 + core)
    parts = [
        dot(columns(s), win[i].reshape(384, WIDTH), NN) for i, s in enumerate(shards_here)
    ]
    partial[...] = parts[0] + parts[1] + parts[2]
    last[...] = columns((1 - zh) * 2 + 1 - core)
    lane = lax.broadcasted_iota(jnp.int32, (1, TOK), 1)
    twice = jnp.where(lane & 1 == 0, F32(1), F32(0))
    keys = given.reshape(WIDTH, TILE)
    bias[...] = jnp.concatenate(
        [
            jnp.where(lane < count, twice, F32(LOW)),
            key_bias(keys[pl.ds(TOK, 64), :]),
            jnp.full((1, 64), LOW, F32),
            key_bias(keys[pl.ds(256, FAR), :]),
        ],
        axis=1,
    )


def layer_kernel(
    scal,
    partial,
    last,
    key_bias_row,
    own,
    mate,
    over,
    cross,
    cot,
    out,
    keep,
    send,
    win,
    wqkv,
    wout,
    hid,
    kv,
    attn,
    sems,
):
    count, zh, core = scal[0], scal[1], scal[2]
    places = (zh * 2 + core, zh * 2 + 1 - core, (1 - zh) * 2 + core, (1 - zh) * 2 + 1 - core)
    packs = (own, mate, over, cross)
    moves = [(cross.at[pl.ds(0, 6)], win)]
    moves += [(p.at[pl.ds(6, 9)], wqkv.at[s]) for p, s in zip(packs, places)]
    moves += [(p.at[pl.ds(15, 3)], wout.at[s]) for p, s in zip(packs, places)]
    copies = [pltpu.make_async_copy(s, d, sems.at[i]) for i, (s, d) in enumerate(moves)]
    for c in copies:
        c.start()
    copies[0].wait()
    fourth = dot(last[...], win[...].reshape(384, WIDTH), NN)
    hid[...] = (partial[...] + fourth).astype(BF)
    bias = key_bias_row[...]
    for c in copies[1:5]:
        c.wait()
    flat = wqkv.reshape(3 * WIDTH, WIDTH)
    kv[...] = dot(flat[pl.ds(WIDTH, 2 * WIDTH), :], hid[...], NT).astype(BF)
    own_hid = hid[pl.ds(0, TOK), :]
    for h in range(HEADS):
        q = dot(own_hid, flat[pl.ds(h * HEAD, HEAD), :], NT).astype(BF)
        s = dot(q, kv[pl.ds(h * HEAD, HEAD), :], NN) * F32(SCALE) + bias
        p = jnp.exp2(s - jnp.max(s, axis=1, keepdims=True))
        o = dot(p.astype(BF), kv[pl.ds(WIDTH + h * HEAD, HEAD), :], NT)
        o = o / jnp.sum(p, axis=1, keepdims=True)
        attn[pl.ds(h * HEAD, HEAD), :] = o.T.astype(BF)
    cotangent = cot[...]
    token = lax.broadcasted_iota(jnp.int32, (192, TOK), 1)
    for which, target in ((core, keep), (1 - core, send)):
        for half in range(2):
            start = pl.multiple_of(half * 384 + which * 192, 192)
            block = attn[pl.ds(start, 192), :]
            block = jnp.where(token < count, block, jnp.zeros_like(block))
            part = dot(block, cotangent, NN)
            for r in range(8):
                for c in range(2):
                    target[r * 2 + c, half] = part[r * 24 : r * 24 + 24, c * 384 : c * 384 + 384].astype(
                        target.dtype
                    )
    for c in copies[5:]:
        c.wait()
    out[...] = dot(wout.reshape(WIDTH, WIDTH)[...], attn[...], NN).T


ANY = pl.BlockSpec(memory_space=pl.ANY)
VMEM = pl.BlockSpec(memory_space=pltpu.VMEM)
SMEM = pl.BlockSpec(memory_space=pltpu.SMEM)


def room(mebibytes):
    return pltpu.CompilerParams(vmem_limit_bytes=mebibytes * 1024 * 1024)


def prepare_kernel(scal, rows, w_in, w_qkv, w_out, own, ahead, even, sems):
    count, zh, at, line = scal[0], scal[1], scal[3], scal[4]
    moves = [
        (w_in, own.at[pl.ds(0, 384)]),
        (w_qkv, own.at[pl.ds(384, 576)]),
        (w_out, own.at[pl.ds(960, 192)]),
    ]
    copies = [pltpu.make_async_copy(s, d, sems.at[i]) for i, (s, d) in enumerate(moves)]
    for c in copies:
        c.start()
    lane = lax.broadcasted_iota(jnp.int32, (1, TILE), 1)
    mark = jnp.where(lane == 0, F32(MARK), F32(0))
    distant = jnp.concatenate(
        [
            jnp.where(DIL * j < count, rows[pl.ds(DIL * j, 16), :].astype(F32)[0:1], mark)
            for j in range(4)
        ],
        axis=0,
    )
    row = lax.broadcasted_iota(jnp.int32, (TOK // 2, TOK), 0)
    source = lax.broadcasted_iota(jnp.int32, (TOK // 2, TOK), 1)
    pick = jnp.where((source == 2 * row) & (source < count), F32(1), F32(0)).astype(BF)
    marks = jnp.where(
        2 * lax.broadcasted_iota(jnp.int32, (TOK // 2, TILE), 0) < count, F32(0), mark
    )
    even[...] = (dot(pick, rows[...], NN) + marks).astype(BF)
    for c in copies:
        c.wait()
    start = pl.multiple_of(at // 16 * 16, 16)
    wide = own[pl.ds(start, 16), :].astype(F32)
    eight = jnp.where(at > start, wide[8:16], wide[0:8])
    start = pl.multiple_of(line // 16 * 16, 16)
    wide = own[pl.ds(start, 16), :].astype(F32)
    single = lax.broadcasted_iota(jnp.int32, (16, WIDTH), 0) == line - start
    ninth = jnp.sum(jnp.where(single, wide, F32(0)), axis=0, keepdims=True)
    far = jnp.concatenate([distant[:, :WIDTH], distant[:, WIDTH:]], axis=0)
    spare = jnp.zeros((2, TOK), F32)
    for half in range(2):
        value = jnp.where(zh == half, far, eight)
        lanes = [value[:, c * TOK : (c + 1) * TOK] for c in range(6)]
        more = [ninth[:, c * TOK : (c + 1) * TOK] for c in range(6)]
        block = jnp.concatenate(lanes + [jnp.concatenate(more + [spare], axis=0)], axis=0)
        ahead[half] = jnp.concatenate([block] * 8, axis=0).astype(BF)


def prepare_call(*operands, interpret=False):
    return pl.pallas_call(
        prepare_kernel,
        out_shape=(
            jax.ShapeDtypeStruct((PACK, WIDTH), BF),
            jax.ShapeDtypeStruct((2, 448, TOK), BF),
            jax.ShapeDtypeStruct((TOK // 2, TILE), BF),
        ),
        in_specs=[SMEM, VMEM] + [ANY] * 3,
        out_specs=(VMEM,) * 3,
        scratch_shapes=[pltpu.SemaphoreType.DMA((3,))],
        compiler_params=room(62),
        interpret=interpret,
    )(*operands)


def split_kernel(scal, line, payload):
    zh = scal[1]
    ours, theirs = line[zh], line[1 - zh]
    target = lax.broadcasted_iota(jnp.int32, (64, 448), 0)
    source = lax.broadcasted_iota(jnp.int32, (64, 448), 1)
    piece = target // 8 * 56 + (target & 7)
    ordered = (target & 31) // 4 * 56 + target // 32 * 4 + (target & 3)
    rest = (target & 7) * 56 + 48
    columns = []
    for c in range(6):
        picks = [
            jnp.where(source == origin, F32(1), F32(0)).astype(BF)
            for origin in (piece + 8 * c, ordered + 8 * c, rest + c)
        ]
        columns.append(
            jnp.concatenate(
                [
                    dot(picks[0], theirs, NN),
                    dot(picks[2], theirs, NN)[0:8],
                    dot(picks[1], ours, NN),
                ],
                axis=0,
            )
        )
    both = jnp.concatenate(columns, axis=1).astype(BF)
    for i in range(16):
        payload[i] = both


def split_call(*operands, interpret=False):
    return pl.pallas_call(
        split_kernel,
        out_shape=jax.ShapeDtypeStruct((16, 136, WIDTH), BF),
        in_specs=[SMEM, VMEM],
        out_specs=VMEM,
        compiler_params=room(16),
        interpret=interpret,
    )(*operands)


def begin_call(*operands, interpret=False):
    return pl.pallas_call(
        begin_kernel,
        out_shape=(
            jax.ShapeDtypeStruct((WIDTH, WIDTH), F32),
            jax.ShapeDtypeStruct((WIDTH, 384), BF),
            jax.ShapeDtypeStruct((1, WIDTH), F32),
        ),
        in_specs=[SMEM] + [ANY] * 6,
        out_specs=(VMEM,) * 3,
        scratch_shapes=[
            pltpu.VMEM((24, 32, TILE), BF),
            pltpu.VMEM((3, 6, 64, WIDTH), BF),
            pltpu.SemaphoreType.DMA((7,)),
        ],
        compiler_params=room(32),
        interpret=interpret,
    )(*operands)


def layer_call(*operands, interpret=False):
    part = jax.ShapeDtypeStruct((16, 2, 24, 384), F32)
    sent = jax.ShapeDtypeStruct((16, 2, 24, 384), BF)
    return pl.pallas_call(
        layer_kernel,
        out_shape=(jax.ShapeDtypeStruct((TOK, WIDTH), F32), part, sent),
        in_specs=[SMEM] + [VMEM] * 3 + [ANY] * 4 + [VMEM],
        out_specs=(VMEM,) * 3,
        scratch_shapes=[
            pltpu.VMEM((6, 64, WIDTH), BF),
            pltpu.VMEM((4, 9, 64, WIDTH), BF),
            pltpu.VMEM((4, 3, 64, WIDTH), BF),
            pltpu.VMEM((WIDTH, WIDTH), BF),
            pltpu.VMEM((2 * WIDTH, WIDTH), BF),
            pltpu.VMEM((WIDTH, TOK), BF),
            pltpu.SemaphoreType.DMA((9,)),
        ],
        compiler_params=room(40),
        interpret=interpret,
    )(*operands)


def spread(block, axes, size):
    return lax.all_to_all(
        jnp.broadcast_to(block[None], (size,) + block.shape), axes, 0, 0, tiled=True
    )


def swap(value, axis):
    return lax.ppermute(value, axis, [(0, 1), (1, 0)])


def shards(tiles, counts, w_in, w_qkv, w_out, cotangent):
    rows = tiles[0]
    count = counts[0, 0]
    yx = lax.axis_index("y") * 4 + lax.axis_index("x")
    zl = lax.axis_index("zl")
    zh, core = lax.axis_index("zh"), lax.axis_index("core")
    w_out = w_out.T
    piece = yx * 72
    scal = jnp.stack([count, zh, core, piece + zl * 8, piece + 64 + zl]).astype(jnp.int32)
    own, ahead, even = prepare_call(scal, rows, w_in, w_qkv.T, w_out)
    line = lax.all_to_all(ahead.reshape(16, 56, TOK), Z, 0, 0, tiled=True)
    mate = swap(own, "core")
    partner = lax.ppermute(even, "zl", [(i, i ^ 1) for i in range(8)])
    line, mate, partner = lax.optimization_barrier((line.reshape(2, 448, TOK), mate, partner))
    got = lax.all_to_all(split_call(scal, line), YX, 0, 0, tiled=True)
    over, far = got[:, :72].reshape(18, 64, WIDTH), got[:, 72:]
    cross = swap(over, "core")
    own, mate = own.reshape(18, 64, WIDTH), mate.reshape(18, 64, WIDTH)
    state = begin_call(
        scal, rows.reshape(4, 32, TILE), partner.reshape(2, 32, TILE), own, mate, over, far
    )
    out, keep, send = layer_call(scal, *state, own, mate, over, cross, cotangent[0])
    pair = (keep + swap(send, "core").astype(F32)).astype(BF)
    plane = lax.all_to_all(pair, YX, 0, 0, tiled=True)
    plane = jnp.sum(plane.astype(F32), axis=0).astype(BF)
    column = jnp.broadcast_to(plane[:, None], (2, 8, 24, 384)).reshape(16, 24, 384)
    column = lax.all_to_all(column, Z, 0, 0, tiled=True)
    total = jnp.sum(column.astype(F32), axis=0)
    whole = spread(total.astype(BF), YX, 16).astype(F32)
    grad = whole.reshape(8, 2, 24, 384).transpose(0, 2, 1, 3).reshape(192, WIDTH)
    return (out[None], grad)


def solution(mesh):
    fine = Mesh(mesh.devices.reshape(4, 4, 8, 2, 2), ("y", "x", "zl", "zh", "core"))
    seq, slide = YX + ("zl",), ("zh", "core")
    placed = (
        P(slide, seq, None),
        P(slide, seq),
        P(slide, None),
        P(None, slide),
        P(None, slide),
        P(slide, seq, None),
    )
    return jax.shard_map(
        shards,
        mesh=fine,
        in_specs=placed,
        out_specs=(P(slide, seq, None), P(slide, None)),
        check_vma=False,
    )
```

```python
import jax
import jax.numpy as jnp
from jax import lax
from jax.experimental import pallas as pl
from jax.experimental.pallas import tpu as pltpu
from jax.sharding import Mesh
from jax.sharding import PartitionSpec as P

WIDTH = 768
TILE = 1536
HEADS = 16
HEAD = 48
DIL = 32
TOK = 128
FAR = 512
PACK = 1152
YX = ("y", "x")
Z = ("zh", "zl")
NT = (((1,), (1,)), ((), ()))
NN = (((1,), (0,)), ((), ()))
BF = jnp.bfloat16
F32 = jnp.float32
MARK = 64.0
LOW = -1e30
SCALE = HEAD**-0.5 / 0.6931471805599453


def dot(a, b, dims):
    return lax.dot_general(a, b, dims, preferred_element_type=F32)


def key_bias(block):
    lane = lax.broadcasted_iota(jnp.int32, (16, TOK), 1)
    pick = jnp.where(lane == 0, F32(1), F32(0)).astype(BF)
    return jnp.where(dot(pick, block[:, :TOK], NT)[0:1] > MARK / 2, F32(LOW), F32(0))


def begin_kernel(scal, rows, partner, own, mate, over, far, partial, last, bias, given, win, sems):
    count, zh, core = scal[0], scal[1], scal[2]
    moves = [
        (own.at[pl.ds(0, 6)], win.at[0]),
        (mate.at[pl.ds(0, 6)], win.at[1]),
        (over.at[pl.ds(0, 6)], win.at[2]),
        (rows, given.at[pl.ds(0, 4)]),
        (partner, given.at[pl.ds(4, 2)]),
        (far.at[:, pl.ds(0, 32)], given.at[pl.ds(8, 16), :, pl.ds(0, WIDTH)]),
        (far.at[:, pl.ds(32, 32)], given.at[pl.ds(8, 16), :, pl.ds(WIDTH, WIDTH)]),
    ]
    copies = [pltpu.make_async_copy(s, d, sems.at[i]) for i, (s, d) in enumerate(moves)]
    for c in copies:
        c.start()
    given[pl.ds(6, 2)] = jnp.zeros((2, 32, TILE), BF)
    for c in copies:
        c.wait()

    def columns(shard):
        start = pl.multiple_of(shard * 384, 384)
        return given[:, :, pl.ds(start, 384)].reshape(WIDTH, 384)

    shards_here = (zh * 2 + core, zh * 2 + 1 - core, (1 - zh) * 2 + core)
    parts = [
        dot(columns(s), win[i].reshape(384, WIDTH), NN) for i, s in enumerate(shards_here)
    ]
    partial[...] = parts[0] + parts[1] + parts[2]
    last[...] = columns((1 - zh) * 2 + 1 - core)
    lane = lax.broadcasted_iota(jnp.int32, (1, TOK), 1)
    twice = jnp.where(lane & 1 == 0, F32(1), F32(0))
    keys = given.reshape(WIDTH, TILE)
    bias[...] = jnp.concatenate(
        [
            jnp.where(lane < count, twice, F32(LOW)),
            key_bias(keys[pl.ds(TOK, 64), :]),
            jnp.full((1, 64), LOW, F32),
            key_bias(keys[pl.ds(256, FAR), :]),
        ],
        axis=1,
    )


def layer_kernel(
    scal,
    partial,
    last,
    key_bias_row,
    own,
    mate,
    over,
    cross,
    cot,
    out,
    keep,
    send,
    win,
    wqkv,
    wout,
    hid,
    kv,
    attn,
    sems,
):
    count, zh, core = scal[0], scal[1], scal[2]
    places = (zh * 2 + core, zh * 2 + 1 - core, (1 - zh) * 2 + core, (1 - zh) * 2 + 1 - core)
    packs = (own, mate, over, cross)
    moves = [(cross.at[pl.ds(0, 6)], win)]
    moves += [(p.at[pl.ds(6, 9)], wqkv.at[s]) for p, s in zip(packs, places)]
    moves += [(p.at[pl.ds(15, 3)], wout.at[s]) for p, s in zip(packs, places)]
    copies = [pltpu.make_async_copy(s, d, sems.at[i]) for i, (s, d) in enumerate(moves)]
    for c in copies:
        c.start()
    copies[0].wait()
    fourth = dot(last[...], win[...].reshape(384, WIDTH), NN)
    hid[...] = (partial[...] + fourth).astype(BF)
    bias = key_bias_row[...]
    for c in copies[1:5]:
        c.wait()
    flat = wqkv.reshape(3 * WIDTH, WIDTH)
    kv[...] = dot(flat[pl.ds(WIDTH, 2 * WIDTH), :], hid[...], NT).astype(BF)
    own_hid = hid[pl.ds(0, TOK), :]
    for h in range(HEADS):
        q = dot(own_hid, flat[pl.ds(h * HEAD, HEAD), :], NT).astype(BF)
        s = dot(q, kv[pl.ds(h * HEAD, HEAD), :], NN) * F32(SCALE) + bias
        p = jnp.exp2(s - jnp.max(s, axis=1, keepdims=True))
        o = dot(p.astype(BF), kv[pl.ds(WIDTH + h * HEAD, HEAD), :], NT)
        o = o / jnp.sum(p, axis=1, keepdims=True)
        attn[pl.ds(h * HEAD, HEAD), :] = o.T.astype(BF)
    cotangent = cot[...]
    token = lax.broadcasted_iota(jnp.int32, (192, TOK), 1)
    for which, target in ((core, keep), (1 - core, send)):
        for half in range(2):
            start = pl.multiple_of(half * 384 + which * 192, 192)
            block = attn[pl.ds(start, 192), :]
            block = jnp.where(token < count, block, jnp.zeros_like(block))
            part = dot(block, cotangent, NN)
            for r in range(8):
                for c in range(2):
                    target[r * 2 + c, half] = part[r * 24 : r * 24 + 24, c * 384 : c * 384 + 384].astype(
                        target.dtype
                    )
    for c in copies[5:]:
        c.wait()
    out[...] = dot(wout.reshape(WIDTH, WIDTH)[...], attn[...], NN).T


ANY = pl.BlockSpec(memory_space=pl.ANY)
VMEM = pl.BlockSpec(memory_space=pltpu.VMEM)
SMEM = pl.BlockSpec(memory_space=pltpu.SMEM)


def room(mebibytes):
    return pltpu.CompilerParams(vmem_limit_bytes=mebibytes * 1024 * 1024)


def prepare_kernel(scal, rows, w_in, w_qkv, w_out, own, ahead, even, sems):
    count, zh, at, line = scal[0], scal[1], scal[3], scal[4]
    moves = [
        (w_in, own.at[pl.ds(0, 384)]),
        (w_qkv, own.at[pl.ds(384, 576)]),
        (w_out, own.at[pl.ds(960, 192)]),
    ]
    copies = [pltpu.make_async_copy(s, d, sems.at[i]) for i, (s, d) in enumerate(moves)]
    for c in copies:
        c.start()
    lane = lax.broadcasted_iota(jnp.int32, (1, TILE), 1)
    mark = jnp.where(lane == 0, F32(MARK), F32(0))
    distant = jnp.concatenate(
        [
            jnp.where(DIL * j < count, rows[pl.ds(DIL * j, 16), :].astype(F32)[0:1], mark)
            for j in range(4)
        ],
        axis=0,
    )
    row = lax.broadcasted_iota(jnp.int32, (TOK // 2, TOK), 0)
    source = lax.broadcasted_iota(jnp.int32, (TOK // 2, TOK), 1)
    pick = jnp.where((source == 2 * row) & (source < count), F32(1), F32(0)).astype(BF)
    marks = jnp.where(
        2 * lax.broadcasted_iota(jnp.int32, (TOK // 2, TILE), 0) < count, F32(0), mark
    )
    even[...] = (dot(pick, rows[...], NN) + marks).astype(BF)
    for c in copies:
        c.wait()
    start = pl.multiple_of(at // 16 * 16, 16)
    wide = own[pl.ds(start, 16), :].astype(F32)
    eight = jnp.where(at > start, wide[8:16], wide[0:8])
    start = pl.multiple_of(line // 16 * 16, 16)
    wide = own[pl.ds(start, 16), :].astype(F32)
    single = lax.broadcasted_iota(jnp.int32, (16, WIDTH), 0) == line - start
    ninth = jnp.sum(jnp.where(single, wide, F32(0)), axis=0, keepdims=True)
    far = jnp.concatenate([distant[:, :WIDTH], distant[:, WIDTH:]], axis=0)
    spare = jnp.zeros((2, TOK), F32)
    for half in range(2):
        value = jnp.where(zh == half, far, eight)
        lanes = [value[:, c * TOK : (c + 1) * TOK] for c in range(6)]
        more = [ninth[:, c * TOK : (c + 1) * TOK] for c in range(6)]
        block = jnp.concatenate(lanes + [jnp.concatenate(more + [spare], axis=0)], axis=0)
        ahead[half] = jnp.concatenate([block] * 8, axis=0).astype(BF)


def prepare_call(*operands, interpret=False):
    return pl.pallas_call(
        prepare_kernel,
        out_shape=(
            jax.ShapeDtypeStruct((PACK, WIDTH), BF),
            jax.ShapeDtypeStruct((2, 448, TOK), BF),
            jax.ShapeDtypeStruct((TOK // 2, TILE), BF),
        ),
        in_specs=[SMEM, VMEM] + [ANY] * 3,
        out_specs=(VMEM,) * 3,
        scratch_shapes=[pltpu.SemaphoreType.DMA((3,))],
        compiler_params=room(62),
        interpret=interpret,
    )(*operands)


def split_kernel(scal, line, payload):
    zh = scal[1]
    ours, theirs = line[zh], line[1 - zh]
    target = lax.broadcasted_iota(jnp.int32, (64, 448), 0)
    source = lax.broadcasted_iota(jnp.int32, (64, 448), 1)
    piece = target // 8 * 56 + (target & 7)
    ordered = (target & 31) // 4 * 56 + target // 32 * 4 + (target & 3)
    rest = (target & 7) * 56 + 48
    columns = []
    for c in range(6):
        picks = [
            jnp.where(source == origin, F32(1), F32(0)).astype(BF)
            for origin in (piece + 8 * c, ordered + 8 * c, rest + c)
        ]
        columns.append(
            jnp.concatenate(
                [
                    dot(picks[0], theirs, NN),
                    dot(picks[2], theirs, NN)[0:8],
                    dot(picks[1], ours, NN),
                ],
                axis=0,
            )
        )
    both = jnp.concatenate(columns, axis=1).astype(BF)
    for i in range(16):
        payload[i] = both


def split_call(*operands, interpret=False):
    return pl.pallas_call(
        split_kernel,
        out_shape=jax.ShapeDtypeStruct((16, 136, WIDTH), BF),
        in_specs=[SMEM, VMEM],
        out_specs=VMEM,
        compiler_params=room(16),
        interpret=interpret,
    )(*operands)


def begin_call(*operands, interpret=False):
    return pl.pallas_call(
        begin_kernel,
        out_shape=(
            jax.ShapeDtypeStruct((WIDTH, WIDTH), F32),
            jax.ShapeDtypeStruct((WIDTH, 384), BF),
            jax.ShapeDtypeStruct((1, WIDTH), F32),
        ),
        in_specs=[SMEM] + [ANY] * 6,
        out_specs=(VMEM,) * 3,
        scratch_shapes=[
            pltpu.VMEM((24, 32, TILE), BF),
            pltpu.VMEM((3, 6, 64, WIDTH), BF),
            pltpu.SemaphoreType.DMA((7,)),
        ],
        compiler_params=room(32),
        interpret=interpret,
    )(*operands)


def layer_call(*operands, interpret=False):
    part = jax.ShapeDtypeStruct((16, 2, 24, 384), F32)
    sent = jax.ShapeDtypeStruct((16, 2, 24, 384), BF)
    return pl.pallas_call(
        layer_kernel,
        out_shape=(jax.ShapeDtypeStruct((TOK, WIDTH), F32), part, sent),
        in_specs=[SMEM] + [VMEM] * 3 + [ANY] * 4 + [VMEM],
        out_specs=(VMEM,) * 3,
        scratch_shapes=[
            pltpu.VMEM((6, 64, WIDTH), BF),
            pltpu.VMEM((4, 9, 64, WIDTH), BF),
            pltpu.VMEM((4, 3, 64, WIDTH), BF),
            pltpu.VMEM((WIDTH, WIDTH), BF),
            pltpu.VMEM((2 * WIDTH, WIDTH), BF),
            pltpu.VMEM((WIDTH, TOK), BF),
            pltpu.SemaphoreType.DMA((9,)),
        ],
        compiler_params=room(40),
        interpret=interpret,
    )(*operands)


def spread(block, axes, size):
    return lax.all_to_all(
        jnp.broadcast_to(block[None], (size,) + block.shape), axes, 0, 0, tiled=True
    )


def swap(value, axis):
    return lax.ppermute(value, axis, [(0, 1), (1, 0)])


def shards(tiles, counts, w_in, w_qkv, w_out, cotangent):
    rows = tiles[0]
    count = counts[0, 0]
    yx = lax.axis_index("y") * 4 + lax.axis_index("x")
    zl = lax.axis_index("zl")
    zh, core = lax.axis_index("zh"), lax.axis_index("core")
    w_out = w_out.T
    piece = yx * 72
    scal = jnp.stack([count, zh, core, piece + zl * 8, piece + 64 + zl]).astype(jnp.int32)
    own, ahead, even = prepare_call(scal, rows, w_in, w_qkv.T, w_out)
    line = lax.all_to_all(ahead.reshape(16, 56, TOK), Z, 0, 0, tiled=True)
    mate = swap(own, "core")
    partner = lax.ppermute(even, "zl", [(i, i ^ 1) for i in range(8)])
    line, mate, partner = lax.optimization_barrier((line.reshape(2, 448, TOK), mate, partner))
    got = lax.all_to_all(split_call(scal, line), YX, 0, 0, tiled=True)
    over, far = got[:, :72].reshape(18, 64, WIDTH), got[:, 72:]
    cross = swap(over, "core")
    own, mate = own.reshape(18, 64, WIDTH), mate.reshape(18, 64, WIDTH)
    state = begin_call(
        scal, rows.reshape(4, 32, TILE), partner.reshape(2, 32, TILE), own, mate, over, far
    )
    out, keep, send = layer_call(scal, *state, own, mate, over, cross, cotangent[0])
    pair = (keep + swap(send, "core").astype(F32)).astype(BF)
    plane = lax.all_to_all(pair, YX, 0, 0, tiled=True)
    plane = jnp.sum(plane.astype(F32), axis=0).astype(BF)
    column = jnp.broadcast_to(plane[:, None], (2, 8, 24, 384)).reshape(16, 24, 384)
    column = lax.all_to_all(column, Z, 0, 0, tiled=True)
    total = jnp.sum(column.astype(F32), axis=0)
    whole = spread(total.astype(BF), YX, 16).reshape(8, 2, 24, 384)
    grad = jnp.concatenate([whole[:, 0], whole[:, 1]], axis=2).astype(F32).reshape(192, WIDTH)
    return (out[None], grad)


def solution(mesh):
    fine = Mesh(mesh.devices.reshape(4, 4, 8, 2, 2), ("y", "x", "zl", "zh", "core"))
    seq, slide = YX + ("zl",), ("zh", "core")
    placed = (
        P(slide, seq, None),
        P(slide, seq),
        P(slide, None),
        P(None, slide),
        P(None, slide),
        P(slide, seq, None),
    )
    return jax.shard_map(
        shards,
        mesh=fine,
        in_specs=placed,
        out_specs=(P(slide, seq, None), P(slide, None)),
        check_vma=False,
    )
```
